256 devices in a mesh: slab: 8 (over x, core), panel: 32 (over y, z).
Axes of the slice: x: 4, y: 4, z: 8, core: 2. Of those that a mesh axis runs over, the one named last changes fastest.
Arguments:
- ranges: float32 [8, 4, 1024, 1024], P('slab', None, 'panel'), may hold values from -1.5 to 1.5
- pattern: int32 [8, 4, 16, 16], P('slab'), may hold values 0 or 1
Outputs:
- combined: float32 [8, 4, 1024, 1024], P('slab', None, 'panel')
The draws below stay inside these ranges and needn't reach their ends.
All inputs are finite; a program needn't handle non-finite values. No bound on the sum of `pattern` on one device may be relied on, other than what follows from the above.
Results may differ from the reference program's by a relative error of at most 0.01.
Values may be sent and summed in bfloat16 or wider, within the bound.
No kernel may reach another device: no remote copies, remote signals or barrier semaphores. Data moves between devices by JAX's collectives and lax.ppermute only.
A program may use at most 64 MiB of HBM per device.

```python
import math
import jax
import jax.numpy as jnp
from jax import lax

M = 1024
BLK = 64
NS_ITERS = 2
LEVELS = 2
GROUPS = 8
NB = 16


def draw_ranges(key, part):
    noise_key = jax.random.fold_in(key, 0)
    sign_key = jax.random.fold_in(key, 1)
    size_key = jax.random.fold_in(key, 2)
    turn_key = jax.random.fold_in(key, 4)
    spread_vals = jnp.clip(jax.random.normal(noise_key, (GROUPS, 4, M, M), jnp.float32), -6.0, 6.0)
    off_part = spread_vals * (0.25 / math.sqrt(M))
    reflect_sign = jnp.where(jax.random.bernoulli(sign_key, 0.5, (GROUPS, M)), 1.0, -1.0)
    carry_sign = jnp.where(jax.random.bernoulli(turn_key, 0.5, (GROUPS, M)), 1.0, -1.0)
    reflect = jax.random.uniform(size_key, (GROUPS, M), jnp.float32, 0.4, 0.7)
    carry = jnp.sqrt(1.0 - reflect * reflect)
    diag_vals = jnp.stack([reflect_sign * reflect, carry_sign * carry, carry_sign * carry, -reflect_sign * reflect], axis=1)
    diagonal = jnp.eye(M, dtype=jnp.float32)[None, None, :, :] * diag_vals[:, :, :, None]
    return (off_part + diagonal).astype(jnp.float32)


def set_ends(values, own_key, least, top_value):
    extent = values.shape
    spot = [jax.random.randint(jax.random.fold_in(own_key, axis), (), 0, extent[axis]) for axis in range(len(extent))]
    values = values.at[tuple(spot)].set(least)
    longest = extent.index(max(extent))
    spot[longest] = (spot[longest] + 1) % extent[longest]
    return values.at[tuple(spot)].set(top_value)


def setup_inputs(seed: int = 0) -> dict:
    arg_keys = jax.random.split(jax.random.key(seed), 3)
    return {
        "ranges": draw_ranges(jax.random.fold_in(arg_keys[2], 71), 0),
        "pattern": set_ends((jax.random.randint(arg_keys[1], (GROUPS, 4, NB, NB), 0, 4) < 3).astype(jnp.int32), jax.random.fold_in(arg_keys[1], 1), 0, 1),
    }


def to_half(values):
    return values.astype(jnp.bfloat16)


def multiply(left, right):
    return jnp.dot(to_half(left), to_half(right), preferred_element_type=jnp.float32)


def star(head, tail):
    head_top, head_up, head_down, head_bottom = head[0], head[1], head[2], head[3]
    tail_top, tail_up, tail_down, tail_bottom = tail[0], tail[1], tail[2], tail[3]
    identity = jnp.eye(M, dtype=jnp.float32)
    loop_term = multiply(tail_top, head_bottom)
    loop_kept = lax.optimization_barrier(to_half(loop_term)).astype(jnp.float32)
    defect = identity - loop_kept
    guess = identity + loop_kept
    for newton_step in range(2, NS_ITERS + 1):
        guess = 2.0 * guess - multiply(multiply(guess, defect), guess)
    lifted = multiply(head_up, guess)
    joint_up = multiply(lifted, tail_up)
    bounce = multiply(tail_top, head_down)
    joint_top = head_top + multiply(lifted, bounce)
    reach = multiply(tail_down, head_bottom)
    through = multiply(reach, guess)
    joint_down = multiply(tail_down, head_down) + multiply(through, bounce)
    joint_bottom = tail_bottom + multiply(reach, tail_up) + multiply(multiply(through, loop_term), tail_up)
    return jnp.stack([joint_top, joint_up, joint_down, joint_bottom])


def reference(ranges, pattern):
    block_mask = jnp.repeat(jnp.repeat(pattern.astype(jnp.float32), BLK, axis=2), BLK, axis=3)
    merged = [ranges[group_id] * block_mask[group_id] for group_id in range(GROUPS)]
    for tree_level in range(LEVELS):
        span_size = 2 ** tree_level
        outcome = list(merged)
        for low_group in range(GROUPS):
            if (low_group // span_size) % 2 == 0:
                result = star(merged[low_group], merged[low_group + span_size])
                outcome[low_group] = result
                outcome[low_group + span_size] = result
        merged = outcome
    return jnp.stack(merged)
```

```python
import functools
import jax
import jax.numpy as jnp
from jax import lax
from jax.experimental import pallas as pl
from jax.experimental.pallas import tpu as pltpu
from jax.sharding import PartitionSpec as P

M = 1024
BLK = 64
LEVELS = 2
NX, NC, NY, NZ = 4, 2, 4, 8
AXES = ("slab", "panel")
TILE = 256


def device(x, c, y, z):
    return ((x % NX) * NC + c) * NY * NZ + (y % NY) * NZ + z % NZ


def route(move):
    pairs = []
    for x in range(NX):
        for c in range(NC):
            for y in range(NY):
                for z in range(NZ):
                    target = move(x, c, y, z)
                    if target is not None:
                        pairs.append((device(x, c, y, z), device(*target)))
    return pairs


def send(block, move):
    return lax.ppermute(block, AXES, route(move))


def step(sign, core0=None, core1=None):
    def move(x, c, y, z):
        axis = core0 if c == 0 else core1
        if axis is None:
            return None
        return (x, c, y + sign, z) if axis == "y" else (x, c, y, z + sign)

    return move


def gather(block):
    s1p = send(block, step(1, "y", "z"))
    s1m = send(block, step(-1, "y", "z"))
    s2p = send(s1p, step(1, "y", "z"))
    s2m = send(s1m, step(-1, None, "z"))
    wide0 = jnp.concatenate([block, s1p, s1m, s2p])
    h1p = send(wide0, step(1, "z", None))
    h1m = send(wide0, step(-1, "z", None))
    s3p = send(s2p, step(1, None, "z"))
    s3m = send(s2m, step(-1, None, "z"))
    s4p = send(s3p, step(1, None, "z"))
    wide1 = jnp.concatenate([block, s1p, s1m, s2p, s2m, s3p, s3m, s4p])
    g1p = send(wide1, step(1, None, "y"))
    g1m = send(wide1, step(-1, None, "y"))
    h2p = send(h1p, step(1, "z", None))
    h2m = send(h1m, step(-1, "z", None))
    h3p = send(h2p, step(1, "z", None))
    h3m = send(h2m, step(-1, "z", None))
    h4p = send(h3p, step(1, "z", None))
    half = g1p.shape[0] // 2
    g2p = send(g1p[:half], step(1, None, "y"))
    g2m = send(g1m[half:], step(-1, None, "y"))
    return [wide0, h1p, h1m, h2p, h2m, h3p, h3m, h4p], [wide1, g1p, g1m, g2p, g2m]


Y_FROM = (0, -1, 1, -2)
Z_FROM = (0, -1, 1, -2, 2, -3, 3, -4)


def place():
    panel = lax.axis_index("panel")
    return panel // NZ, panel % NZ


def row_of(y, z):
    return pl.multiple_of((lax.rem(y + NY, NY) * NZ + lax.rem(z + NZ, NZ)) * 32, 32)


def wide_dot(left, factor, out):
    rows = left.shape[0]

    @pl.loop(0, M // TILE)
    def _(tile):
        cols = pl.ds(pl.multiple_of(tile * TILE, TILE), TILE)
        out[pl.ds(0, rows), cols] = jnp.dot(
            left[...], factor[:, cols], preferred_element_type=jnp.float32
        )


def chain_kernel(where, rows, *refs):
    parts, (out, first, second, left, prod, sums, sem) = refs[:8], refs[8:]
    y, z = where[1], where[2]

    @pl.when(where[0] == 0)
    def _():
        copies = []
        for part, z_from in zip(parts, Z_FROM):
            for k, y_from in enumerate(Y_FROM):
                at = row_of(y + y_from, z + z_from)
                for which, full in enumerate((first, second)):
                    copies.append(
                        pltpu.make_async_copy(
                            part.at[pl.ds(k * 64 + which * 32, 32)], full.at[pl.ds(at, 32)], sem
                        )
                    )
        for copy in copies:
            copy.start()
        for copy in copies:
            copy.wait()
        half = jnp.bfloat16
        down, up = rows[0], rows[1]
        left[pl.ds(0, 32)] = down.astype(half)
        left[pl.ds(32, 32)] = up.astype(half)
        wide_dot(left, second, prod)
        reach = prod[pl.ds(0, 32)]
        left[pl.ds(0, 32)] = reach.astype(half)
        sums[0] = reach
        sums[1] = up
        sums[2] = down
        sums[3] = jnp.zeros((32, M), jnp.float32)

        @pl.loop(0, 4)
        def _(n):
            wide_dot(left, first, prod)
            sums[2] += prod[pl.ds(0, 32)]
            sums[3] += prod[pl.ds(32, 32)]
            left[...] = prod[...].astype(half)
            wide_dot(left, second, prod)
            sums[0] += prod[pl.ds(0, 32)]

            @pl.when(n < 3)
            def _():
                sums[1] += prod[pl.ds(32, 32)]

            left[...] = prod[...].astype(half)

        out[...] = sums[...].astype(half)


def chain(where, rows, parts):
    any_spec = pl.BlockSpec(memory_space=pl.ANY)
    vmem = pl.BlockSpec(memory_space=pltpu.VMEM)
    return pl.pallas_call(
        chain_kernel,
        out_shape=jax.ShapeDtypeStruct((4, 32, M), jnp.bfloat16),
        in_specs=[pl.BlockSpec(memory_space=pltpu.SMEM), vmem] + [any_spec] * 8,
        out_specs=vmem,
        scratch_shapes=[
            pltpu.VMEM((M, M), jnp.bfloat16),
            pltpu.VMEM((M, M), jnp.bfloat16),
            pltpu.VMEM((64, M), jnp.bfloat16),
            pltpu.VMEM((64, M), jnp.float32),
            pltpu.VMEM((4, 32, M), jnp.float32),
            pltpu.SemaphoreType.DMA,
        ],
        compiler_params=pltpu.CompilerParams(vmem_limit_bytes=24 << 20),
        name="chain",
    )(where, rows, *parts)


def finish_kernel(where, lefts, adds, *refs):
    wide, g1p, g1m, g2p, g2m, out, first, second, prod, sem = refs
    y, z = where[1], where[2]

    @pl.when(where[0] == 1)
    def _():
        copies = []
        for k, z_from in enumerate(Z_FROM):
            far = (g2p, k) if k < 4 else (g2m, k - 4)
            for (part, slot), y_from in zip(((wide, k), (g1p, k), (g1m, k), far), Y_FROM):
                at = row_of(y + y_from, z + z_from)
                for which, full in enumerate((first, second)):
                    copies.append(
                        pltpu.make_async_copy(
                            part.at[pl.ds(slot * 64 + which * 32, 32)], full.at[pl.ds(at, 32)], sem
                        )
                    )
        for copy in copies:
            copy.start()
        for copy in copies:
            copy.wait()
        wide_dot(lefts.at[pl.ds(0, 64)], first, prod)
        out[3] = adds[1] + prod[pl.ds(0, 32)]
        out[1] = prod[pl.ds(32, 32)]
        wide_dot(lefts.at[pl.ds(64, 64)], second, prod)
        out[2] = prod[pl.ds(0, 32)]
        out[0] = adds[0] + prod[pl.ds(32, 32)]


def finish(where, lefts, adds, parts):
    any_spec = pl.BlockSpec(memory_space=pl.ANY)
    vmem = pl.BlockSpec(memory_space=pltpu.VMEM)
    return pl.pallas_call(
        finish_kernel,
        out_shape=jax.ShapeDtypeStruct((4, 32, M), jnp.float32),
        in_specs=[pl.BlockSpec(memory_space=pltpu.SMEM), vmem, vmem] + [any_spec] * 5,
        out_specs=vmem,
        scratch_shapes=[
            pltpu.VMEM((M, M), jnp.bfloat16),
            pltpu.VMEM((M, M), jnp.bfloat16),
            pltpu.VMEM((64, M), jnp.float32),
            pltpu.SemaphoreType.DMA,
        ],
        compiler_params=pltpu.CompilerParams(vmem_limit_bytes=24 << 20),
        name="finish",
    )(where, lefts, adds, *parts)


def star(where, core, block, rows, adds):
    parts0, parts1 = gather(block)
    sums = chain(where, rows, parts0)
    lefts = send(sums.reshape(128, M), lambda x, c, y, z: (x, 1, y, z) if c == 0 else None)
    return finish(where, lefts, adds, parts1)


def body(ranges, pattern):
    half = jnp.bfloat16
    slab = lax.axis_index("slab")
    panel = lax.axis_index("panel")
    core = slab % NC
    upper = (slab // NC) % 2 == 1
    where = jnp.stack([core, panel // NZ, panel % NZ]).astype(jnp.int32)
    mask_rows = lax.dynamic_slice_in_dim(pattern[0], panel * 32 // BLK, 1, axis=1)
    mask = jnp.repeat(mask_rows.astype(jnp.float32), BLK, axis=2)
    own = ranges[0] * mask

    other = send(
        jnp.stack([own[0], own[2]]), lambda x, c, y, z: (x, 1 - c, y, z)
    )
    is0 = core == 0
    block = jnp.concatenate(
        [jnp.where(is0, other[0], own[1]), jnp.where(is0, own[3], other[1])]
    ).astype(half)
    rows = jnp.stack([other[1], own[1]])
    adds = jnp.stack([other[0], own[3]])
    joint = star(where, core, block, rows, adds)

    to0 = jnp.where(upper, jnp.stack([joint[0], joint[2]]), jnp.stack([joint[3], joint[1]]))
    to0 = to0.astype(half)
    own0 = send(to0, lambda x, c, y, z: (x, 0, y, z) if c == 1 else None)
    far0 = send(to0, lambda x, c, y, z: (x ^ 1, 0, y, z) if c == 1 else None)
    own1 = jnp.where(upper, jnp.stack([joint[1], joint[3]]), jnp.stack([joint[2], joint[0]]))
    far1 = send(own1, lambda x, c, y, z: (x ^ 1, 1, y, z) if c == 1 else None)
    tail0, head0 = jnp.where(upper, own0, far0), jnp.where(upper, far0, own0)
    tail1, head1 = jnp.where(upper, own1, far1), jnp.where(upper, far1, own1)
    block = jnp.where(
        is0,
        jnp.concatenate([tail0[0], head0[0]]),
        jnp.concatenate([tail1[0], head1[0]]).astype(half),
    )
    rows = jnp.stack([tail0[1], head0[1]]).astype(jnp.float32)
    adds = jnp.stack([head1[1], tail1[1]])
    joint = star(where, core, block, rows, adds)
    shared = send(joint, lambda x, c, y, z: (x, 0, y, z) if c == 1 else None)
    return jnp.where(is0, shared, joint)[None]


def solution(mesh):
    return jax.shard_map(
        body,
        mesh=mesh,
        in_specs=(P("slab", None, "panel", None), P("slab", None, None, None)),
        out_specs=P("slab", None, "panel", None),
        check_vma=False,
    )
```

```python
import jax
import jax.numpy as jnp
from jax import lax
from jax.experimental import pallas as pl
from jax.experimental.pallas import tpu as pltpu
from jax.sharding import PartitionSpec as P

M = 1024
BLK = 64
NX, NC, NY, NZ = 4, 2, 4, 8
AXES = ("slab", "panel")
TILE = 256
SPLIT = 384
PARTS = NZ + NY


def device(x, c, y, z):
    return ((x % NX) * NC + c) * NY * NZ + (y % NY) * NZ + z % NZ


def route(move):
    pairs = []
    for x in range(NX):
        for c in range(NC):
            for y in range(NY):
                for z in range(NZ):
                    target = move(x, c, y, z)
                    if target is not None:
                        pairs.append((device(x, c, y, z), device(*target)))
    return pairs


def send(block, move):
    return lax.ppermute(block, AXES, route(move))


def hop(axis, distance):
    def move(x, c, y, z):
        ahead = distance if c == 0 else -distance
        return (x, c, y + ahead, z) if axis == "y" else (x, c, y, z + ahead)

    return move


def gather(block):
    wide_a, wide_b = block[:, :SPLIT], block[:, SPLIT:]
    for y_distance, z_distance in ((2, 4), (1, 2)):
        more_a, more_b = lax.optimization_barrier(
            (send(wide_a, hop("y", y_distance)), send(wide_b, hop("z", z_distance)))
        )
        wide_a = jnp.concatenate([wide_a, more_a])
        wide_b = jnp.concatenate([wide_b, more_b])
    next_a, more_b = lax.optimization_barrier(
        (send(wide_a, hop("z", 1)), send(wide_b, hop("z", 1)))
    )
    wide_b = jnp.concatenate([wide_b, more_b])
    parts_a, parts_b = [wide_a, next_a], [wide_b]
    for _ in range(NZ - 2):
        parts_a.append(send(parts_a[-1], hop("z", 1)))
    for _ in range(NY - 1):
        parts_b.append(send(parts_b[-1], hop("y", 1)))
    return parts_a, parts_b


Y_BACK = (0, 2, 1, 3)
Z_BACK = (0, 4, 2, 6, 1, 5, 3, 7)


def row_of(y, z):
    return pl.multiple_of((lax.rem(y + 2 * NY, NY) * NZ + lax.rem(z + 2 * NZ, NZ)) * 32, 32)


def order(where, parts, first, second):
    parts_a, parts_b = parts[:NZ], parts[NZ:]
    way, y, z = 1 - 2 * where[0], where[1], where[2]
    for z_back, part in enumerate(parts_a):
        for k, y_back in enumerate(Y_BACK):
            at = pl.ds(row_of(y - way * y_back, z - way * z_back), 32)
            first[at, :SPLIT] = part[pl.ds(k * 64, 32)]
            second[at, :SPLIT] = part[pl.ds(k * 64 + 32, 32)]
    for y_back, part in enumerate(parts_b):
        for k, z_back in enumerate(Z_BACK):
            at = pl.ds(row_of(y - way * y_back, z - way * z_back), 32)
            first[at, SPLIT:] = part[pl.ds(k * 64, 32)]
            second[at, SPLIT:] = part[pl.ds(k * 64 + 32, 32)]


def wide_dot(left, factor, out):
    rows = left.shape[0]

    @pl.loop(0, M // TILE)
    def _(tile):
        cols = pl.ds(pl.multiple_of(tile * TILE, TILE), TILE)
        out[pl.ds(0, rows), cols] = jnp.dot(
            left[...], factor[:, cols], preferred_element_type=jnp.float32
        )


def chain_kernel(where, rows, *refs):
    parts, (out, first, second, left, prod, sums) = refs[:PARTS], refs[PARTS:]

    @pl.when(where[0] == 0)
    def _():
        order(where, parts, first, second)
        half = jnp.bfloat16
        down, up = rows[0], rows[1]
        left[pl.ds(0, 32)] = down.astype(half)
        left[pl.ds(32, 32)] = up.astype(half)
        wide_dot(left, second, prod)
        reach = prod[pl.ds(0, 32)]
        left[pl.ds(0, 32)] = reach.astype(half)
        sums[0] = reach
        sums[1] = up
        sums[2] = down
        sums[3] = jnp.zeros((32, M), jnp.float32)

        @pl.loop(0, 4)
        def _(n):
            wide_dot(left, first, prod)
            sums[2] += prod[pl.ds(0, 32)]
            sums[3] += prod[pl.ds(32, 32)]
            left[...] = prod[...].astype(half)
            wide_dot(left, second, prod)
            sums[0] += prod[pl.ds(0, 32)]

            @pl.when(n < 3)
            def _():
                sums[1] += prod[pl.ds(32, 32)]

            left[...] = prod[...].astype(half)

        out[...] = sums[...].astype(half)


def chain(where, rows, parts):
    vmem = pl.BlockSpec(memory_space=pltpu.VMEM)
    return pl.pallas_call(
        chain_kernel,
        out_shape=jax.ShapeDtypeStruct((4, 32, M), jnp.bfloat16),
        in_specs=[pl.BlockSpec(memory_space=pltpu.SMEM), vmem] + [vmem] * PARTS,
        out_specs=vmem,
        scratch_shapes=[
            pltpu.VMEM((M, M), jnp.bfloat16),
            pltpu.VMEM((M, M), jnp.bfloat16),
            pltpu.VMEM((64, M), jnp.bfloat16),
            pltpu.VMEM((64, M), jnp.float32),
            pltpu.VMEM((4, 32, M), jnp.float32),
        ],
        compiler_params=pltpu.CompilerParams(vmem_limit_bytes=24 << 20),
        name="chain",
    )(where, rows, *parts)


def order_kernel(where, *refs):
    parts, (first, second) = refs[:PARTS], refs[PARTS:]

    @pl.when(where[0] == 1)
    def _():
        order(where, parts, first, second)


def ordered(where, parts):
    vmem = pl.BlockSpec(memory_space=pltpu.VMEM)
    return pl.pallas_call(
        order_kernel,
        out_shape=[jax.ShapeDtypeStruct((M, M), jnp.bfloat16)] * 2,
        in_specs=[pl.BlockSpec(memory_space=pltpu.SMEM)] + [vmem] * PARTS,
        out_specs=[vmem, vmem],
        compiler_params=pltpu.CompilerParams(vmem_limit_bytes=24 << 20),
        name="order",
    )(where, *parts)


def finish_kernel(where, lefts, adds, first, second, out, prod):
    @pl.when(where[0] == 1)
    def _():
        wide_dot(lefts.at[pl.ds(0, 64)], first, prod)
        out[3] = adds[1] + prod[pl.ds(0, 32)]
        out[1] = prod[pl.ds(32, 32)]
        wide_dot(lefts.at[pl.ds(64, 64)], second, prod)
        out[2] = prod[pl.ds(0, 32)]
        out[0] = adds[0] + prod[pl.ds(32, 32)]


def finish(where, lefts, adds, first, second):
    vmem = pl.BlockSpec(memory_space=pltpu.VMEM)
    return pl.pallas_call(
        finish_kernel,
        out_shape=jax.ShapeDtypeStruct((4, 32, M), jnp.float32),
        in_specs=[pl.BlockSpec(memory_space=pltpu.SMEM)] + [vmem] * 4,
        out_specs=vmem,
        scratch_shapes=[pltpu.VMEM((64, M), jnp.float32)],
        compiler_params=pltpu.CompilerParams(vmem_limit_bytes=16 << 20),
        name="finish",
    )(where, lefts, adds, first, second)


def star(where, block, rows, adds):
    parts_a, parts_b = gather(block)
    parts = parts_a + parts_b
    sums = chain(where, rows, parts)
    lefts = send(sums.reshape(128, M), lambda x, c, y, z: (x, 1, y, z) if c == 0 else None)
    return finish(where, lefts, adds, *ordered(where, parts))


def body(ranges, pattern):
    half = jnp.bfloat16
    slab = lax.axis_index("slab")
    panel = lax.axis_index("panel")
    core = slab % NC
    upper = (slab // NC) % 2 == 1
    where = jnp.stack([core, panel // NZ, panel % NZ]).astype(jnp.int32)
    mask_rows = lax.dynamic_slice_in_dim(pattern[0], panel * 32 // BLK, 1, axis=1)
    mask = jnp.repeat(mask_rows.astype(jnp.float32), BLK, axis=2)
    own = ranges[0] * mask

    other = send(
        jnp.stack([own[0], own[2]]), lambda x, c, y, z: (x, 1 - c, y, z)
    )
    is0 = core == 0
    block = jnp.concatenate(
        [jnp.where(is0, other[0], own[1]), jnp.where(is0, own[3], other[1])]
    ).astype(half)
    rows = jnp.stack([other[1], own[1]])
    adds = jnp.stack([other[0], own[3]])
    joint = star(where, block, rows, adds)

    to0 = jnp.where(upper, jnp.stack([joint[0], joint[2]]), jnp.stack([joint[3], joint[1]]))
    to0 = to0.astype(half)
    own0 = send(to0, lambda x, c, y, z: (x, 0, y, z) if c == 1 else None)
    far0 = send(to0, lambda x, c, y, z: (x ^ 1, 0, y, z) if c == 1 else None)
    own1 = jnp.where(upper, jnp.stack([joint[1], joint[3]]), jnp.stack([joint[2], joint[0]]))
    far1 = send(own1.astype(half), lambda x, c, y, z: (x ^ 1, 1, y, z) if c == 1 else None)
    tail0, head0 = jnp.where(upper, own0, far0), jnp.where(upper, far0, own0)
    far1 = far1.astype(jnp.float32)
    tail1, head1 = jnp.where(upper, own1, far1), jnp.where(upper, far1, own1)
    block = jnp.where(
        is0,
        jnp.concatenate([tail0[0], head0[0]]),
        jnp.concatenate([tail1[0], head1[0]]).astype(half),
    )
    rows = jnp.stack([tail0[1], head0[1]]).astype(jnp.float32)
    adds = jnp.stack([head1[1], tail1[1]])
    joint = star(where, block, rows, adds)
    shared = send(joint, lambda x, c, y, z: (x, 0, y, z) if c == 1 else None)
    return jnp.where(is0, shared, joint)[None]


def solution(mesh):
    return jax.shard_map(
        body,
        mesh=mesh,
        in_specs=(P("slab", None, "panel", None), P("slab", None, None, None)),
        out_specs=P("slab", None, "panel", None),
        check_vma=False,
    )
```

```python
import jax
import jax.numpy as jnp
from jax import lax
from jax.experimental import pallas as pl
from jax.experimental.pallas import tpu as pltpu
from jax.sharding import PartitionSpec as P

M = 1024
BLK = 64
NX, NC, NY, NZ = 4, 2, 4, 8
AXES = ("slab", "panel")
SPLIT = 640
PARTS = NZ + NY


def device(x, c, y, z):
    return ((x % NX) * NC + c) * NY * NZ + (y % NY) * NZ + z % NZ


def route(move):
    pairs = []
    for x in range(NX):
        for c in range(NC):
            for y in range(NY):
                for z in range(NZ):
                    target = move(x, c, y, z)
                    if target is not None:
                        pairs.append((device(x, c, y, z), device(*target)))
    return pairs


def send(block, move):
    return lax.ppermute(block, AXES, route(move))


def hop(axis, distance):
    def move(x, c, y, z):
        ahead = distance if c == 0 else -distance
        return (x, c, y + ahead, z) if axis == "y" else (x, c, y, z + ahead)

    return move


def gather(block):
    wide_a, wide_b = block[:, :SPLIT], block[:, SPLIT:]
    wide_a = jnp.concatenate([wide_a] + [send(wide_a, hop("y", d)) for d in Y_BACK[1:]])
    wide_b = jnp.concatenate([wide_b, send(wide_b, hop("z", 4))])
    ahead, behind = send(wide_b, hop("z", 1)), send(wide_b, hop("z", -1))
    wide_b = jnp.concatenate([wide_b, ahead, behind, send(ahead, hop("z", 1))])
    parts_a, parts_b = [wide_a], [wide_b]
    ahead, behind = wide_a, wide_a
    for back in Z_BACK_A[1:]:
        if back > 0:
            ahead = send(ahead, hop("z", 1))
            parts_a.append(ahead)
        else:
            behind = send(behind, hop("z", -1))
            parts_a.append(behind)
    ahead, behind = send(wide_b, hop("y", 1)), send(wide_b, hop("y", -1))
    parts_b += [ahead, behind, send(ahead, hop("y", 1))]
    return parts_a, parts_b


Y_BACK = (0, 1, -1, 2)
Z_BACK_A = (0, 1, -1, 2, -2, 3, -3, 4)
Z_BACK_B = (0, 4, 1, 5, -1, 3, 2, 6)


def row_of(y, z):
    return pl.multiple_of((lax.rem(y + 2 * NY, NY) * NZ + lax.rem(z + 2 * NZ, NZ)) * 32, 32)


def order(where, parts, first, second):
    parts_a, parts_b = parts[:NZ], parts[NZ:]
    way, y, z = 1 - 2 * where[0], where[1], where[2]
    for z_back, part in zip(Z_BACK_A, parts_a):
        for k, y_back in enumerate(Y_BACK):
            at = pl.ds(row_of(y - way * y_back, z - way * z_back), 32)
            first[at, :SPLIT] = part[pl.ds(k * 64, 32)]
            second[at, :SPLIT] = part[pl.ds(k * 64 + 32, 32)]
    for y_back, part in zip(Y_BACK, parts_b):
        for k, z_back in enumerate(Z_BACK_B):
            at = pl.ds(row_of(y - way * y_back, z - way * z_back), 32)
            first[at, SPLIT:] = part[pl.ds(k * 64, 32)]
            second[at, SPLIT:] = part[pl.ds(k * 64 + 32, 32)]


def wide_dot(left, factor, out):
    out[pl.ds(0, left.shape[0])] = jnp.dot(
        left[...], factor[...], preferred_element_type=jnp.float32
    )


def chain_kernel(where, rows, *refs):
    parts, (out, first, second, left, prod, sums) = refs[:PARTS], refs[PARTS:]

    @pl.when(where[0] == 0)
    def _():
        order(where, parts, first, second)
        half = jnp.bfloat16
        down, up = rows[0], rows[1]
        left[pl.ds(0, 32)] = down.astype(half)
        left[pl.ds(32, 32)] = up.astype(half)
        wide_dot(left, second, prod)
        reach = prod[pl.ds(0, 32)]
        left[pl.ds(0, 32)] = reach.astype(half)
        sums[0] = reach
        sums[1] = up
        sums[2] = down
        sums[3] = jnp.zeros((32, M), jnp.float32)

        @pl.loop(0, 4)
        def _(n):
            wide_dot(left, first, prod)
            sums[2] += prod[pl.ds(0, 32)]
            sums[3] += prod[pl.ds(32, 32)]
            left[...] = prod[...].astype(half)
            wide_dot(left, second, prod)
            sums[0] += prod[pl.ds(0, 32)]

            @pl.when(n < 3)
            def _():
                sums[1] += prod[pl.ds(32, 32)]

            left[...] = prod[...].astype(half)

        out[...] = sums[...].astype(half)


def chain(where, rows, parts):
    vmem = pl.BlockSpec(memory_space=pltpu.VMEM)
    return pl.pallas_call(
        chain_kernel,
        out_shape=jax.ShapeDtypeStruct((4, 32, M), jnp.bfloat16),
        in_specs=[pl.BlockSpec(memory_space=pltpu.SMEM), vmem] + [vmem] * PARTS,
        out_specs=vmem,
        scratch_shapes=[
            pltpu.VMEM((M, M), jnp.bfloat16),
            pltpu.VMEM((M, M), jnp.bfloat16),
            pltpu.VMEM((64, M), jnp.bfloat16),
            pltpu.VMEM((64, M), jnp.float32),
            pltpu.VMEM((4, 32, M), jnp.float32),
        ],
        compiler_params=pltpu.CompilerParams(vmem_limit_bytes=24 << 20),
        name="chain",
    )(where, rows, *parts)


def order_kernel(where, *refs):
    parts, (first, second) = refs[:PARTS], refs[PARTS:]

    @pl.when(where[0] == 1)
    def _():
        order(where, parts, first, second)


def ordered(where, parts):
    vmem = pl.BlockSpec(memory_space=pltpu.VMEM)
    return pl.pallas_call(
        order_kernel,
        out_shape=[jax.ShapeDtypeStruct((M, M), jnp.bfloat16)] * 2,
        in_specs=[pl.BlockSpec(memory_space=pltpu.SMEM)] + [vmem] * PARTS,
        out_specs=[vmem, vmem],
        compiler_params=pltpu.CompilerParams(vmem_limit_bytes=24 << 20),
        name="order",
    )(where, *parts)


def finish_kernel(where, lefts, adds, first, second, out, prod):
    @pl.when(where[0] == 1)
    def _():
        wide_dot(lefts.at[pl.ds(0, 64)], first, prod)
        out[3] = adds[1] + prod[pl.ds(0, 32)]
        out[1] = prod[pl.ds(32, 32)]
        wide_dot(lefts.at[pl.ds(64, 64)], second, prod)
        out[2] = prod[pl.ds(0, 32)]
        out[0] = adds[0] + prod[pl.ds(32, 32)]


def finish(where, lefts, adds, first, second):
    vmem = pl.BlockSpec(memory_space=pltpu.VMEM)
    return pl.pallas_call(
        finish_kernel,
        out_shape=jax.ShapeDtypeStruct((4, 32, M), jnp.float32),
        in_specs=[pl.BlockSpec(memory_space=pltpu.SMEM)] + [vmem] * 4,
        out_specs=vmem,
        scratch_shapes=[pltpu.VMEM((64, M), jnp.float32)],
        compiler_params=pltpu.CompilerParams(vmem_limit_bytes=16 << 20),
        name="finish",
    )(where, lefts, adds, first, second)


def star(where, block, rows, adds):
    parts_a, parts_b = gather(block)
    parts = parts_a + parts_b
    sums = chain(where, rows, parts)
    lefts = send(sums.reshape(128, M), lambda x, c, y, z: (x, 1, y, z) if c == 0 else None)
    return finish(where, lefts, adds, *ordered(where, parts))


def body(ranges, pattern):
    half = jnp.bfloat16
    slab = lax.axis_index("slab")
    panel = lax.axis_index("panel")
    core = slab % NC
    upper = (slab // NC) % 2 == 1
    where = jnp.stack([core, panel // NZ, panel % NZ]).astype(jnp.int32)
    mask_rows = lax.dynamic_slice_in_dim(pattern[0], panel * 32 // BLK, 1, axis=1)
    mask = jnp.repeat(mask_rows.astype(jnp.float32), BLK, axis=2)
    own = ranges[0] * mask

    other = send(
        jnp.stack([own[0], own[2]]), lambda x, c, y, z: (x, 1 - c, y, z)
    )
    is0 = core == 0
    block = jnp.concatenate(
        [jnp.where(is0, other[0], own[1]), jnp.where(is0, own[3], other[1])]
    ).astype(half)
    rows = jnp.stack([other[1], own[1]])
    adds = jnp.stack([other[0], own[3]])
    joint = star(where, block, rows, adds)

    to0 = jnp.where(upper, jnp.stack([joint[0], joint[2]]), jnp.stack([joint[3], joint[1]]))
    to0 = to0.astype(half)
    own0 = send(to0, lambda x, c, y, z: (x, 0, y, z) if c == 1 else None)
    far0 = send(to0, lambda x, c, y, z: (x ^ 1, 0, y, z) if c == 1 else None)
    own1 = jnp.where(upper, jnp.stack([joint[1], joint[3]]), jnp.stack([joint[2], joint[0]]))
    far1 = send(own1.astype(half), lambda x, c, y, z: (x ^ 1, 1, y, z) if c == 1 else None)
    tail0, head0 = jnp.where(upper, own0, far0), jnp.where(upper, far0, own0)
    far1 = far1.astype(jnp.float32)
    tail1, head1 = jnp.where(upper, own1, far1), jnp.where(upper, far1, own1)
    block = jnp.where(
        is0,
        jnp.concatenate([tail0[0], head0[0]]),
        jnp.concatenate([tail1[0], head1[0]]).astype(half),
    )
    rows = jnp.stack([tail0[1], head0[1]]).astype(jnp.float32)
    adds = jnp.stack([head1[1], tail1[1]])
    joint = star(where, block, rows, adds)
    shared = send(joint, lambda x, c, y, z: (x, 0, y, z) if c == 1 else None)
    return jnp.where(is0, shared, joint)[None]


def solution(mesh):
    return jax.shard_map(
        body,
        mesh=mesh,
        in_specs=(P("slab", None, "panel", None), P("slab", None, None, None)),
        out_specs=P("slab", None, "panel", None),
        check_vma=False,
    )
```

```python
import functools
import jax
import jax.numpy as jnp
from jax import lax
from jax.experimental import pallas as pl
from jax.experimental.pallas import tpu as pltpu
from jax.sharding import PartitionSpec as P

M = 1024
BLK = 64
NX, NC, NY, NZ = 4, 2, 4, 8
AXES = ("slab", "panel")
SPLIT = 640
PARTS = NZ + NY


def device(x, c, y, z):
    return ((x % NX) * NC + c) * NY * NZ + (y % NY) * NZ + z % NZ


def route(move):
    pairs = []
    for x in range(NX):
        for c in range(NC):
            for y in range(NY):
                for z in range(NZ):
                    target = move(x, c, y, z)
                    if target is not None:
                        pairs.append((device(x, c, y, z), device(*target)))
    return pairs


def send(block, move):
    return lax.ppermute(block, AXES, route(move))


def hop(axis, distance):
    def move(x, c, y, z):
        ahead = distance if c == 0 else -distance
        return (x, c, y + ahead, z) if axis == "y" else (x, c, y, z + ahead)

    return move


def gather(block):
    wide_a, wide_b = block[:, :SPLIT], block[:, SPLIT:]
    wide_a = jnp.concatenate([wide_a] + [send(wide_a, hop("y", d)) for d in Y_BACK[1:]])
    wide_b = jnp.concatenate([wide_b, send(wide_b, hop("z", 4))])
    ahead, behind = send(wide_b, hop("z", 1)), send(wide_b, hop("z", -1))
    wide_b = jnp.concatenate([wide_b, ahead, behind, send(ahead, hop("z", 1))])
    parts_a, parts_b = [wide_a], [wide_b]
    ahead, behind = wide_a, wide_a
    for back in Z_BACK_A[1:]:
        if back > 0:
            ahead = send(ahead, hop("z", 1))
            parts_a.append(ahead)
        else:
            behind = send(behind, hop("z", -1))
            parts_a.append(behind)
    ahead, behind = send(wide_b, hop("y", 1)), send(wide_b, hop("y", -1))
    parts_b += [ahead, behind, send(ahead, hop("y", 1))]
    return parts_a, parts_b


Y_BACK = (0, 1, -1, 2)
Z_BACK_A = (0, 1, -1, 2, -2, 3, -3, 4)
Z_BACK_B = (0, 4, 1, 5, -1, 3, 2, 6)


def row_of(y, z):
    return pl.multiple_of((lax.rem(y + 2 * NY, NY) * NZ + lax.rem(z + 2 * NZ, NZ)) * 32, 32)


def order(where, parts, first, second):
    parts_a, parts_b = parts[:NZ], parts[NZ:]
    way, y, z = 1 - 2 * where[0], where[1], where[2]
    for z_back, part in zip(Z_BACK_A, parts_a):
        for k, y_back in enumerate(Y_BACK):
            at = pl.ds(row_of(y - way * y_back, z - way * z_back), 32)
            first[at, :SPLIT] = part[pl.ds(k * 64, 32)]
            second[at, :SPLIT] = part[pl.ds(k * 64 + 32, 32)]
    for y_back, part in zip(Y_BACK, parts_b):
        for k, z_back in enumerate(Z_BACK_B):
            at = pl.ds(row_of(y - way * y_back, z - way * z_back), 32)
            first[at, SPLIT:] = part[pl.ds(k * 64, 32)]
            second[at, SPLIT:] = part[pl.ds(k * 64 + 32, 32)]


def wide_dot(left, factor, out):
    out[pl.ds(0, left.shape[0])] = jnp.dot(
        left[...], factor[...], preferred_element_type=jnp.float32
    )


def mask_kernel(where, pattern, ranges, keep, give):
    block_row = pl.ds(lax.div(where[1] * NZ + where[2], BLK // 32), 1)
    count = M // BLK
    spread = (
        lax.broadcasted_iota(jnp.int32, (count, M), 0)
        == lax.div(lax.broadcasted_iota(jnp.int32, (count, M), 1), BLK)
    ).astype(jnp.bfloat16)
    for b, (out, at) in enumerate(((keep, 0), (give, 0), (keep, 1), (give, 1))):
        present = pattern[b, block_row, :].astype(jnp.float32).astype(jnp.bfloat16)
        mask = jnp.dot(present, spread, preferred_element_type=jnp.float32)
        out[at] = ranges[b] * mask


VMEM = pl.BlockSpec(memory_space=pltpu.VMEM)
SMEM = pl.BlockSpec(memory_space=pltpu.SMEM)


def masked(where, pattern, ranges):
    return pl.pallas_call(
        mask_kernel,
        out_shape=[jax.ShapeDtypeStruct((2, 32, M), jnp.float32)] * 2,
        in_specs=[SMEM, VMEM, VMEM],
        out_specs=[VMEM, VMEM],
        compiler_params=pltpu.CompilerParams(vmem_limit_bytes=8 << 20),
        name="masked",
    )(where, pattern, ranges)


def chain_kernel(where, keep, other, *refs):
    parts, (out, first, second, left, prod, sums) = refs[:PARTS], refs[PARTS:]
    order(where, parts, first, second)

    @pl.when(where[0] == 1)
    def _():
        half = jnp.bfloat16
        down, up = keep[1].astype(jnp.float32), other[0].astype(jnp.float32)
        left[pl.ds(0, 32)] = down.astype(half)
        left[pl.ds(32, 32)] = up.astype(half)
        wide_dot(left, second, prod)
        reach = prod[pl.ds(0, 32)]
        left[pl.ds(0, 32)] = reach.astype(half)
        sums[pl.ds(0, 32)] = reach
        sums[pl.ds(32, 32)] = up
        sums[pl.ds(64, 32)] = down
        sums[pl.ds(96, 32)] = jnp.zeros((32, M), jnp.float32)

        @pl.loop(0, 4)
        def _(n):
            wide_dot(left, first, prod)
            sums[pl.ds(64, 64)] += prod[...]
            left[...] = prod[...].astype(half)
            wide_dot(left, second, prod)
            sums[pl.ds(0, 32)] += prod[pl.ds(0, 32)]

            @pl.when(n < 3)
            def _():
                sums[pl.ds(32, 32)] += prod[pl.ds(32, 32)]

            left[...] = prod[...].astype(half)

        out[...] = sums[...].astype(half)


def chain(where, keep, other, parts):
    return pl.pallas_call(
        chain_kernel,
        out_shape=[
            jax.ShapeDtypeStruct((128, M), jnp.bfloat16),
            jax.ShapeDtypeStruct((M, M), jnp.bfloat16),
            jax.ShapeDtypeStruct((M, M), jnp.bfloat16),
        ],
        in_specs=[SMEM] + [VMEM] * (2 + PARTS),
        out_specs=[VMEM] * 3,
        scratch_shapes=[
            pltpu.VMEM((64, M), jnp.bfloat16),
            pltpu.VMEM((64, M), jnp.float32),
            pltpu.VMEM((128, M), jnp.float32),
        ],
        compiler_params=pltpu.CompilerParams(vmem_limit_bytes=20 << 20),
        name="chain",
    )(where, keep, other, *parts)


def finish_kernel(last, where, lefts, keep, other, first, second, *refs):
    outs, prod = refs[:-1], refs[-1]

    @pl.when(where[0] == 0)
    def _():
        wide_dot(lefts.at[pl.ds(0, 64)], first, prod.at[0])
        wide_dot(lefts.at[pl.ds(64, 64)], second, prod.at[1])
        top = keep[0].astype(jnp.float32) + prod[1, pl.ds(32, 32)]
        up = prod[0, pl.ds(32, 32)]
        down = prod[1, pl.ds(0, 32)]
        bottom = other[1].astype(jnp.float32) + prod[0, pl.ds(0, 32)]
        if last:
            for at, block in enumerate((top, up, down, bottom)):
                outs[0][at] = block
            return
        mine, mine_half, rest_half = outs
        for odd, pair, rest in ((0, (top, down), (up, bottom)), (1, (up, bottom), (top, down))):

            @pl.when(where[3] == odd)
            def _(pair=pair, rest=rest):
                for at in range(2):
                    mine[at] = pair[at]
                    mine_half[at] = pair[at].astype(jnp.bfloat16)
                    rest_half[at] = rest[at].astype(jnp.bfloat16)


def finish(last, where, lefts, keep, other, first, second):
    pair = (2, 32, M)
    if last:
        shapes = [jax.ShapeDtypeStruct((4, 32, M), jnp.float32)]
    else:
        shapes = [
            jax.ShapeDtypeStruct(pair, kind) for kind in (jnp.float32, jnp.bfloat16, jnp.bfloat16)
        ]
    return pl.pallas_call(
        functools.partial(finish_kernel, last),
        out_shape=shapes,
        in_specs=[SMEM] + [VMEM] * 5,
        out_specs=[VMEM] * len(shapes),
        scratch_shapes=[pltpu.VMEM((2, 64, M), jnp.float32)],
        compiler_params=pltpu.CompilerParams(vmem_limit_bytes=16 << 20),
        name="finish",
    )(where, lefts, keep, other, first, second)


def star(last, where, keep, other):
    block = jnp.where(
        where[0] == 1,
        jnp.concatenate([keep[0], other[1]]),
        jnp.concatenate([other[0], keep[1]]),
    ).astype(jnp.bfloat16)
    parts_a, parts_b = gather(block)
    sums, first, second = chain(where, keep, other, parts_a + parts_b)
    lefts = send(sums, lambda x, c, y, z: (x, 0, y, z) if c == 1 else None)
    return finish(last, where, lefts, keep, other, first, second)


def body(ranges, pattern):
    slab = lax.axis_index("slab")
    panel = lax.axis_index("panel")
    core, odd = slab % NC, (slab // NC) % 2
    where = jnp.stack([core, panel // NZ, panel % NZ, odd]).astype(jnp.int32)

    keep, give = masked(where, pattern[0], ranges[0])
    other = send(give, lambda x, c, y, z: (x, 1 - c, y, z))
    mine, mine_half, rest_half = star(False, where, keep, other)

    near = send(rest_half, lambda x, c, y, z: (x, 1, y, z) if c == 0 else None)
    across = send(rest_half, lambda x, c, y, z: (x ^ 1, 1, y, z) if c == 0 else None)
    far = send(mine_half, lambda x, c, y, z: (x ^ 1, 0, y, z) if c == 0 else None)
    this = jnp.where(core == 0, mine, across.astype(jnp.float32))
    that = jnp.where(core == 0, far, near).astype(jnp.float32)
    keep, other = jnp.where(odd == 1, that, this), jnp.where(odd == 1, this, that)
    (joint,) = star(True, where, keep, other)
    shared = send(joint, lambda x, c, y, z: (x, 1, y, z) if c == 0 else None)
    return jnp.where(core == 1, shared, joint)[None]


def solution(mesh):
    return jax.shard_map(
        body,
        mesh=mesh,
        in_specs=(P("slab", None, "panel", None), P("slab", None, None, None)),
        out_specs=P("slab", None, "panel", None),
        check_vma=False,
    )
```

```python
import functools
import jax
import jax.numpy as jnp
from jax import lax
from jax.experimental import pallas as pl
from jax.experimental.pallas import tpu as pltpu
from jax.sharding import PartitionSpec as P

M = 1024
BLK = 64
NX, NC, NY, NZ = 4, 2, 4, 8
AXES = ("slab", "panel")
PARTS = 8


def device(x, c, y, z):
    return ((x % NX) * NC + c) * NY * NZ + (y % NY) * NZ + z % NZ


def route(move):
    pairs = []
    for x in range(NX):
        for c in range(NC):
            for y in range(NY):
                for z in range(NZ):
                    target = move(x, c, y, z)
                    if target is not None:
                        pairs.append((device(x, c, y, z), device(*target)))
    return pairs


def send(block, move):
    return lax.ppermute(block, AXES, route(move))


def hop(axis, distance):
    def move(x, c, y, z):
        ahead = distance if c == 0 else -distance
        return (x, c, y + ahead, z) if axis == "y" else (x, c, y, z + ahead)

    return move


def gather(block):
    pair = send(block, hop("z", NZ // 2))
    wide_a = jnp.concatenate([block[:32], pair[:32]])
    wide_b = jnp.concatenate([block[32:], pair[32:]])
    ahead, behind = send(wide_a, hop("y", 1)), send(wide_a, hop("y", -1))
    wide_a = jnp.concatenate([wide_a, ahead, behind, send(wide_a, hop("y", 2))])
    ahead, behind = send(wide_b, hop("z", 1)), send(wide_b, hop("z", -1))
    wide_b = jnp.concatenate([wide_b, ahead, behind, send(ahead, hop("z", 1))])
    ahead, behind = send(wide_a, hop("z", 1)), send(wide_a, hop("z", -1))
    parts_a = [wide_a, ahead, behind, send(ahead, hop("z", 1))]
    ahead, behind = send(wide_b, hop("y", 1)), send(wide_b, hop("y", -1))
    parts_b = [wide_b, ahead, behind, send(ahead, hop("y", 1))]
    return parts_a, parts_b


BACK = (0, 1, -1, 2)


def row_of(y, z):
    return pl.multiple_of((lax.rem(y + 2 * NY, NY) * NZ + lax.rem(z + 2 * NZ, NZ)) * 32, 32)


def order(where, parts, first, second):
    way, y, z = 1 - 2 * where[0], where[1], where[2]
    for part_a, part_b, outer in zip(parts[:4], parts[4:], BACK):
        for k, inner in enumerate(BACK):
            for j, far in enumerate((0, NZ // 2)):
                piece = pl.ds((2 * k + j) * 32, 32)
                at = pl.ds(row_of(y - way * inner, z - way * (outer + far)), 32)
                first[at] = part_a[piece]
                at = pl.ds(row_of(y - way * outer, z - way * (inner + far)), 32)
                second[at] = part_b[piece]


def wide_dot(left, factor, out):
    out[pl.ds(0, left.shape[0])] = jnp.dot(
        left[...], factor[...], preferred_element_type=jnp.float32
    )


def mask_kernel(where, pattern_hbm, ranges_hbm, keep, give, pattern, ranges, sems):
    copies = [
        pltpu.make_async_copy(pattern_hbm, pattern, sems.at[0]),
        pltpu.make_async_copy(ranges_hbm, ranges, sems.at[1]),
    ]
    for copy in copies:
        copy.start()
    for copy in copies:
        copy.wait()
    block_row = pl.ds(lax.div(where[1] * NZ + where[2], BLK // 32), 1)
    count = M // BLK
    spread = (
        lax.broadcasted_iota(jnp.int32, (count, M), 0)
        == lax.div(lax.broadcasted_iota(jnp.int32, (count, M), 1), BLK)
    ).astype(jnp.bfloat16)
    for b, (out, at) in enumerate(((keep, 0), (give, 0), (keep, 1), (give, 1))):
        present = pattern[b, block_row, :].astype(jnp.float32).astype(jnp.bfloat16)
        mask = jnp.dot(present, spread, preferred_element_type=jnp.float32)
        out[at] = ranges[b] * mask


VMEM = pl.BlockSpec(memory_space=pltpu.VMEM)
SMEM = pl.BlockSpec(memory_space=pltpu.SMEM)


def masked(where, pattern, ranges):
    return pl.pallas_call(
        mask_kernel,
        out_shape=[jax.ShapeDtypeStruct((2, 32, M), jnp.float32)] * 2,
        in_specs=[SMEM] + [pl.BlockSpec(memory_space=pl.ANY)] * 2,
        out_specs=[VMEM, VMEM],
        scratch_shapes=[
            pltpu.VMEM((4, M // BLK, M // BLK), jnp.int32),
            pltpu.VMEM((4, 32, M), jnp.float32),
            pltpu.SemaphoreType.DMA((2,)),
        ],
        compiler_params=pltpu.CompilerParams(vmem_limit_bytes=8 << 20),
        name="masked",
    )(where, pattern, ranges)


def chain_kernel(where, keep, other, *refs):
    parts, (out, first, second, left, prod, sums) = refs[:PARTS], refs[PARTS:]
    order(where, parts, first, second)

    @pl.when(where[0] == 1)
    def _():
        half = jnp.bfloat16
        down, up = keep[1].astype(jnp.float32), other[0].astype(jnp.float32)
        left[pl.ds(0, 32)] = down.astype(half)
        left[pl.ds(32, 32)] = up.astype(half)
        wide_dot(left, second, prod)
        reach = prod[pl.ds(0, 32)]
        left[pl.ds(0, 32)] = reach.astype(half)
        sums[pl.ds(0, 32)] = reach
        sums[pl.ds(32, 32)] = up
        sums[pl.ds(64, 32)] = down
        sums[pl.ds(96, 32)] = jnp.zeros((32, M), jnp.float32)

        @pl.loop(0, 4)
        def _(n):
            wide_dot(left, first, prod)
            sums[pl.ds(64, 64)] += prod[...]
            left[...] = prod[...].astype(half)
            wide_dot(left, second, prod)
            sums[pl.ds(0, 32)] += prod[pl.ds(0, 32)]

            @pl.when(n < 3)
            def _():
                sums[pl.ds(32, 32)] += prod[pl.ds(32, 32)]

            left[...] = prod[...].astype(half)

        out[...] = sums[...].astype(half)


def chain(where, keep, other, parts):
    return pl.pallas_call(
        chain_kernel,
        out_shape=[
            jax.ShapeDtypeStruct((128, M), jnp.bfloat16),
            jax.ShapeDtypeStruct((M, M), jnp.bfloat16),
            jax.ShapeDtypeStruct((M, M), jnp.bfloat16),
        ],
        in_specs=[SMEM] + [VMEM] * (2 + PARTS),
        out_specs=[VMEM] * 3,
        scratch_shapes=[
            pltpu.VMEM((64, M), jnp.bfloat16),
            pltpu.VMEM((64, M), jnp.float32),
            pltpu.VMEM((128, M), jnp.float32),
        ],
        compiler_params=pltpu.CompilerParams(vmem_limit_bytes=20 << 20),
        name="chain",
    )(where, keep, other, *parts)


def finish_kernel(last, where, lefts, keep, other, first, second, *refs):
    outs, prod = refs[:-1], refs[-1]

    @pl.when(where[0] == 0)
    def _():
        wide_dot(lefts.at[pl.ds(0, 64)], first, prod.at[0])
        wide_dot(lefts.at[pl.ds(64, 64)], second, prod.at[1])
        top = keep[0].astype(jnp.float32) + prod[1, pl.ds(32, 32)]
        up = prod[0, pl.ds(32, 32)]
        down = prod[1, pl.ds(0, 32)]
        bottom = other[1].astype(jnp.float32) + prod[0, pl.ds(0, 32)]
        if last:
            for at, block in enumerate((top, up, down, bottom)):
                outs[0][at] = block
            return
        mine, mine_half, rest_half = outs
        for odd, pair, rest in ((0, (top, down), (up, bottom)), (1, (up, bottom), (top, down))):

            @pl.when(where[3] == odd)
            def _(pair=pair, rest=rest):
                for at in range(2):
                    mine[at] = pair[at]
                    mine_half[at] = pair[at].astype(jnp.bfloat16)
                    rest_half[at] = rest[at].astype(jnp.bfloat16)


def finish(last, where, lefts, keep, other, first, second):
    pair = (2, 32, M)
    if last:
        shapes = [jax.ShapeDtypeStruct((4, 32, M), jnp.float32)]
    else:
        shapes = [
            jax.ShapeDtypeStruct(pair, kind) for kind in (jnp.float32, jnp.bfloat16, jnp.bfloat16)
        ]
    return pl.pallas_call(
        functools.partial(finish_kernel, last),
        out_shape=shapes,
        in_specs=[SMEM] + [VMEM] * 5,
        out_specs=[VMEM] * len(shapes),
        scratch_shapes=[pltpu.VMEM((2, 64, M), jnp.float32)],
        compiler_params=pltpu.CompilerParams(vmem_limit_bytes=16 << 20),
        name="finish",
    )(where, lefts, keep, other, first, second)


def star(last, where, keep, other):
    block = jnp.where(
        where[0] == 1,
        jnp.concatenate([keep[0], other[1]]),
        jnp.concatenate([other[0], keep[1]]),
    ).astype(jnp.bfloat16)
    parts_a, parts_b = gather(block)
    sums, first, second = chain(where, keep, other, parts_a + parts_b)
    lefts = send(sums, lambda x, c, y, z: (x, 0, y, z) if c == 1 else None)
    return finish(last, where, lefts, keep, other, first, second)


def body(ranges, pattern):
    slab = lax.axis_index("slab")
    panel = lax.axis_index("panel")
    core, odd = slab % NC, (slab // NC) % 2
    where = jnp.stack([core, panel // NZ, panel % NZ, odd]).astype(jnp.int32)

    keep, give = masked(where, pattern[0], ranges[0])
    other = send(give, lambda x, c, y, z: (x, 1 - c, y, z))
    mine, mine_half, rest_half = star(False, where, keep, other)

    near = send(rest_half, lambda x, c, y, z: (x, 1, y, z) if c == 0 else None)
    across = send(rest_half, lambda x, c, y, z: (x ^ 1, 1, y, z) if c == 0 else None)
    far = send(mine_half, lambda x, c, y, z: (x ^ 1, 0, y, z) if c == 0 else None)
    this = jnp.where(core == 0, mine, across.astype(jnp.float32))
    that = jnp.where(core == 0, far, near).astype(jnp.float32)
    keep, other = jnp.where(odd == 1, that, this), jnp.where(odd == 1, this, that)
    (joint,) = star(True, where, keep, other)
    shared = send(joint, lambda x, c, y, z: (x, 1, y, z) if c == 0 else None)
    return jnp.where(core == 1, shared, joint)[None]


def solution(mesh):
    return jax.shard_map(
        body,
        mesh=mesh,
        in_specs=(P("slab", None, "panel", None), P("slab", None, None, None)),
        out_specs=P("slab", None, "panel", None),
        check_vma=False,
    )
```

```python
import functools
import jax
import jax.numpy as jnp
from jax import lax
from jax.experimental import pallas as pl
from jax.experimental.pallas import tpu as pltpu
from jax.sharding import PartitionSpec as P

M = 1024
BLK = 64
NX, NC, NY, NZ = 4, 2, 4, 8
AXES = ("slab", "panel")
PARTS = 8


def device(x, c, y, z):
    return ((x % NX) * NC + c) * NY * NZ + (y % NY) * NZ + z % NZ


def route(move):
    pairs = []
    for x in range(NX):
        for c in range(NC):
            for y in range(NY):
                for z in range(NZ):
                    target = move(x, c, y, z)
                    if target is not None:
                        pairs.append((device(x, c, y, z), device(*target)))
    return pairs


def send(block, move):
    return lax.ppermute(block, AXES, route(move))


def hop(axis, distance):
    def move(x, c, y, z):
        ahead = distance if c == 0 else -distance
        return (x, c, y + ahead, z) if axis == "y" else (x, c, y, z + ahead)

    return move


def gather(block):
    pair = send(block, hop("z", NZ // 2))
    wide_a = jnp.concatenate([block[:32], pair[:32]])
    wide_b = jnp.concatenate([block[32:], pair[32:]])
    ahead, behind = send(wide_a, hop("y", 1)), send(wide_a, hop("y", -1))
    wide_a = jnp.concatenate([wide_a, ahead, behind, send(wide_a, hop("y", 2))])
    ahead, behind = send(wide_b, hop("z", 1)), send(wide_b, hop("z", -1))
    wide_b = jnp.concatenate([wide_b, ahead, behind, send(ahead, hop("z", 1))])
    wide_a, wide_b = lax.optimization_barrier((wide_a, wide_b))
    ahead, behind = send(wide_a, hop("z", 1)), send(wide_a, hop("z", -1))
    parts_a = [wide_a, ahead, behind, send(ahead, hop("z", 1))]
    ahead, behind = send(wide_b, hop("y", 1)), send(wide_b, hop("y", -1))
    parts_b = [wide_b, ahead, behind, send(ahead, hop("y", 1))]
    return parts_a, parts_b


BACK = (0, 1, -1, 2)


def row_of(y, z):
    return pl.multiple_of((lax.rem(y + 2 * NY, NY) * NZ + lax.rem(z + 2 * NZ, NZ)) * 32, 32)


def order(where, parts, first, second):
    way, y, z = 1 - 2 * where[0], where[1], where[2]
    for part_a, part_b, outer in zip(parts[:4], parts[4:], BACK):
        for k, inner in enumerate(BACK):
            for j, far in enumerate((0, NZ // 2)):
                piece = pl.ds((2 * k + j) * 32, 32)
                at = pl.ds(row_of(y - way * inner, z - way * (outer + far)), 32)
                first[at] = part_a[piece]
                at = pl.ds(row_of(y - way * outer, z - way * (inner + far)), 32)
                second[at] = part_b[piece]


def wide_dot(left, factor, out):
    out[pl.ds(0, left.shape[0])] = jnp.dot(
        left[...], factor[...], preferred_element_type=jnp.float32
    )


def mask_kernel(where, pattern_hbm, ranges_hbm, keep, give, pattern, ranges, sems):
    copies = [
        pltpu.make_async_copy(pattern_hbm, pattern, sems.at[0]),
        pltpu.make_async_copy(ranges_hbm, ranges, sems.at[1]),
    ]
    for copy in copies:
        copy.start()
    for copy in copies:
        copy.wait()
    block_row = pl.ds(lax.div(where[1] * NZ + where[2], BLK // 32), 1)
    count = M // BLK
    spread = (
        lax.broadcasted_iota(jnp.int32, (count, M), 0)
        == lax.div(lax.broadcasted_iota(jnp.int32, (count, M), 1), BLK)
    ).astype(jnp.bfloat16)
    for b, (out, at) in enumerate(((keep, 0), (give, 0), (keep, 1), (give, 1))):
        present = pattern[b, block_row, :].astype(jnp.float32).astype(jnp.bfloat16)
        mask = jnp.dot(present, spread, preferred_element_type=jnp.float32)
        out[at] = ranges[b] * mask


VMEM = pl.BlockSpec(memory_space=pltpu.VMEM)
SMEM = pl.BlockSpec(memory_space=pltpu.SMEM)


def masked(where, pattern, ranges):
    return pl.pallas_call(
        mask_kernel,
        out_shape=[jax.ShapeDtypeStruct((2, 32, M), jnp.float32)] * 2,
        in_specs=[SMEM] + [pl.BlockSpec(memory_space=pl.ANY)] * 2,
        out_specs=[VMEM, VMEM],
        scratch_shapes=[
            pltpu.VMEM((4, M // BLK, M // BLK), jnp.int32),
            pltpu.VMEM((4, 32, M), jnp.float32),
            pltpu.SemaphoreType.DMA((2,)),
        ],
        compiler_params=pltpu.CompilerParams(vmem_limit_bytes=8 << 20),
        name="masked",
    )(where, pattern, ranges)


def chain_kernel(where, keep, other, *refs):
    parts, (out, first, second, left, prod, sums) = refs[:PARTS], refs[PARTS:]
    order(where, parts, first, second)

    @pl.when(where[0] == 1)
    def _():
        half = jnp.bfloat16
        down, up = keep[1].astype(jnp.float32), other[0].astype(jnp.float32)
        left[pl.ds(0, 32)] = down.astype(half)
        left[pl.ds(32, 32)] = up.astype(half)
        wide_dot(left, second, prod)
        reach = prod[pl.ds(0, 32)]
        left[pl.ds(0, 32)] = reach.astype(half)
        sums[pl.ds(0, 32)] = reach
        sums[pl.ds(32, 32)] = up
        sums[pl.ds(64, 32)] = down
        sums[pl.ds(96, 32)] = jnp.zeros((32, M), jnp.float32)

        @pl.loop(0, 4)
        def _(n):
            wide_dot(left, first, prod)
            sums[pl.ds(64, 64)] += prod[...]
            left[...] = prod[...].astype(half)
            wide_dot(left, second, prod)
            sums[pl.ds(0, 32)] += prod[pl.ds(0, 32)]

            @pl.when(n < 3)
            def _():
                sums[pl.ds(32, 32)] += prod[pl.ds(32, 32)]

            left[...] = prod[...].astype(half)

        out[...] = sums[...].astype(half)


def chain(where, keep, other, parts):
    return pl.pallas_call(
        chain_kernel,
        out_shape=[
            jax.ShapeDtypeStruct((128, M), jnp.bfloat16),
            jax.ShapeDtypeStruct((M, M), jnp.bfloat16),
            jax.ShapeDtypeStruct((M, M), jnp.bfloat16),
        ],
        in_specs=[SMEM] + [VMEM] * (2 + PARTS),
        out_specs=[VMEM] * 3,
        scratch_shapes=[
            pltpu.VMEM((64, M), jnp.bfloat16),
            pltpu.VMEM((64, M), jnp.float32),
            pltpu.VMEM((128, M), jnp.float32),
        ],
        compiler_params=pltpu.CompilerParams(vmem_limit_bytes=20 << 20),
        name="chain",
    )(where, keep, other, *parts)


def finish_kernel(last, where, lefts, keep, other, first, second, *refs):
    outs, prod = refs[:-1], refs[-1]

    @pl.when(where[0] == 0)
    def _():
        wide_dot(lefts.at[pl.ds(0, 64)], first, prod.at[0])
        wide_dot(lefts.at[pl.ds(64, 64)], second, prod.at[1])
        top = keep[0].astype(jnp.float32) + prod[1, pl.ds(32, 32)]
        up = prod[0, pl.ds(32, 32)]
        down = prod[1, pl.ds(0, 32)]
        bottom = other[1].astype(jnp.float32) + prod[0, pl.ds(0, 32)]
        if last:
            for at, block in enumerate((top, up, down, bottom)):
                outs[0][at] = block
            return
        mine, mine_half, rest_half = outs
        for odd, pair, rest in ((0, (top, down), (up, bottom)), (1, (up, bottom), (top, down))):

            @pl.when(where[3] == odd)
            def _(pair=pair, rest=rest):
                for at in range(2):
                    mine[at] = pair[at]
                    mine_half[at] = pair[at].astype(jnp.bfloat16)
                    rest_half[at] = rest[at].astype(jnp.bfloat16)


def finish(last, where, lefts, keep, other, first, second):
    pair = (2, 32, M)
    if last:
        shapes = [jax.ShapeDtypeStruct((4, 32, M), jnp.float32)]
    else:
        shapes = [
            jax.ShapeDtypeStruct(pair, kind) for kind in (jnp.float32, jnp.bfloat16, jnp.bfloat16)
        ]
    return pl.pallas_call(
        functools.partial(finish_kernel, last),
        out_shape=shapes,
        in_specs=[SMEM] + [VMEM] * 5,
        out_specs=[VMEM] * len(shapes),
        scratch_shapes=[pltpu.VMEM((2, 64, M), jnp.float32)],
        compiler_params=pltpu.CompilerParams(vmem_limit_bytes=16 << 20),
        name="finish",
    )(where, lefts, keep, other, first, second)


def star(last, where, keep, other):
    block = jnp.where(
        where[0] == 1,
        jnp.concatenate([keep[0], other[1]]),
        jnp.concatenate([other[0], keep[1]]),
    ).astype(jnp.bfloat16)
    parts_a, parts_b = gather(block)
    sums, first, second = chain(where, keep, other, parts_a + parts_b)
    lefts = send(sums, lambda x, c, y, z: (x, 0, y, z) if c == 1 else None)
    return finish(last, where, lefts, keep, other, first, second)


def body(ranges, pattern):
    slab = lax.axis_index("slab")
    panel = lax.axis_index("panel")
    core, odd = slab % NC, (slab // NC) % 2
    where = jnp.stack([core, panel // NZ, panel % NZ, odd]).astype(jnp.int32)

    keep, give = masked(where, pattern[0], ranges[0])
    other = send(give, lambda x, c, y, z: (x, 1 - c, y, z))
    mine, mine_half, rest_half = star(False, where, keep, other)

    near = send(rest_half, lambda x, c, y, z: (x, 1, y, z) if c == 0 else None)
    across = send(rest_half, lambda x, c, y, z: (x ^ 1, 1, y, z) if c == 0 else None)
    far = send(mine_half, lambda x, c, y, z: (x ^ 1, 0, y, z) if c == 0 else None)
    this = jnp.where(core == 0, mine, across.astype(jnp.float32))
    that = jnp.where(core == 0, far, near).astype(jnp.float32)
    keep, other = jnp.where(odd == 1, that, this), jnp.where(odd == 1, this, that)
    (joint,) = star(True, where, keep, other)
    shared = send(joint, lambda x, c, y, z: (x, 1, y, z) if c == 0 else None)
    return jnp.where(core == 1, shared, joint)[None]


def solution(mesh):
    return jax.shard_map(
        body,
        mesh=mesh,
        in_specs=(P("slab", None, "panel", None), P("slab", None, None, None)),
        out_specs=P("slab", None, "panel", None),
        check_vma=False,
    )
```

```python
import functools
import jax
import jax.numpy as jnp
from jax import lax
from jax.experimental import pallas as pl
from jax.experimental.pallas import tpu as pltpu
from jax.sharding import PartitionSpec as P

M = 1024
BLK = 64
NX, NC, NY, NZ = 4, 2, 4, 8
AXES = ("slab", "panel")
PARTS = 8


def device(x, c, y, z):
    return ((x % NX) * NC + c) * NY * NZ + (y % NY) * NZ + z % NZ


def route(move):
    pairs = []
    for x in range(NX):
        for c in range(NC):
            for y in range(NY):
                for z in range(NZ):
                    target = move(x, c, y, z)
                    if target is not None:
                        pairs.append((device(x, c, y, z), device(*target)))
    return pairs


def send(block, move):
    return lax.ppermute(block, AXES, route(move))


def hop(axis, distance):
    def move(x, c, y, z):
        ahead = distance if c == 0 else -distance
        return (x, c, y + ahead, z) if axis == "y" else (x, c, y, z + ahead)

    return move


def gather(block):
    pair = send(block, hop("z", NZ // 2))
    wide_a = jnp.concatenate([block[:32], pair[:32]])
    wide_b = jnp.concatenate([block[32:], pair[32:]])
    ahead, behind = send(wide_a, hop("y", 1)), send(wide_a, hop("y", -1))
    wide_a = jnp.concatenate([wide_a, ahead, behind, send(wide_a, hop("y", 2))])
    ahead, behind = send(wide_b, hop("z", 1)), send(wide_b, hop("z", -1))
    wide_b = jnp.concatenate([wide_b, ahead, behind, send(ahead, hop("z", 1))])
    wide_a, wide_b = lax.optimization_barrier((wide_a, wide_b))
    ahead, behind = send(wide_a, hop("z", 1)), send(wide_a, hop("z", -1))
    parts_a = [wide_a, ahead, behind, send(ahead, hop("z", 1))]
    ahead, behind = send(wide_b, hop("y", 1)), send(wide_b, hop("y", -1))
    parts_b = [wide_b, ahead, behind, send(ahead, hop("y", 1))]
    return parts_a, parts_b


BACK = (0, 1, -1, 2)


def row_of(y, z):
    return pl.multiple_of((lax.rem(y + 2 * NY, NY) * NZ + lax.rem(z + 2 * NZ, NZ)) * 32, 32)


def order(where, parts, first, second):
    way, y, z = 1 - 2 * where[0], where[1], where[2]
    for part_a, part_b, outer in zip(parts[:4], parts[4:], BACK):
        for k, inner in enumerate(BACK):
            for j, far in enumerate((0, NZ // 2)):
                piece = pl.ds((2 * k + j) * 32, 32)
                at = pl.ds(row_of(y - way * inner, z - way * (outer + far)), 32)
                first[at] = part_a[piece]
                at = pl.ds(row_of(y - way * outer, z - way * (inner + far)), 32)
                second[at] = part_b[piece]


def wide_dot(left, factor, out):
    out[pl.ds(0, left.shape[0])] = jnp.dot(
        left[...], factor[...], preferred_element_type=jnp.float32
    )


def mask_kernel(where, pattern_hbm, ranges_hbm, keep, give, pattern, ranges, sems):
    copies = [
        pltpu.make_async_copy(pattern_hbm, pattern, sems.at[0]),
        pltpu.make_async_copy(ranges_hbm, ranges, sems.at[1]),
    ]
    for copy in copies:
        copy.start()
    for copy in copies:
        copy.wait()
    block_row = pl.ds(lax.div(where[1] * NZ + where[2], BLK // 32), 1)
    count = M // BLK
    spread = (
        lax.broadcasted_iota(jnp.int32, (count, M), 0)
        == lax.div(lax.broadcasted_iota(jnp.int32, (count, M), 1), BLK)
    ).astype(jnp.bfloat16)
    for b, (out, at) in enumerate(((keep, 0), (give, 0), (keep, 1), (give, 1))):
        present = pattern[b, block_row, :].astype(jnp.float32).astype(jnp.bfloat16)
        mask = jnp.dot(present, spread, preferred_element_type=jnp.float32)
        out[at] = ranges[b] * mask


VMEM = pl.BlockSpec(memory_space=pltpu.VMEM)
SMEM = pl.BlockSpec(memory_space=pltpu.SMEM)


def masked(where, pattern, ranges):
    return pl.pallas_call(
        mask_kernel,
        out_shape=[jax.ShapeDtypeStruct((2, 32, M), jnp.float32)] * 2,
        in_specs=[SMEM] + [pl.BlockSpec(memory_space=pltpu.HBM)] * 2,
        out_specs=[VMEM, VMEM],
        scratch_shapes=[
            pltpu.VMEM((4, M // BLK, M // BLK), jnp.int32),
            pltpu.VMEM((4, 32, M), jnp.float32),
            pltpu.SemaphoreType.DMA((2,)),
        ],
        compiler_params=pltpu.CompilerParams(vmem_limit_bytes=60 << 20),
        name="masked",
    )(where, pattern, ranges)


def chain_kernel(where, keep, other, *refs):
    parts, (out, first, second, left, prod, sums) = refs[:PARTS], refs[PARTS:]
    order(where, parts, first, second)

    @pl.when(where[0] == 1)
    def _():
        half = jnp.bfloat16
        down, up = keep[1].astype(jnp.float32), other[0].astype(jnp.float32)
        left[pl.ds(0, 32)] = down.astype(half)
        left[pl.ds(32, 32)] = up.astype(half)
        wide_dot(left, second, prod)
        reach = prod[pl.ds(0, 32)]
        left[pl.ds(0, 32)] = reach.astype(half)
        sums[pl.ds(0, 32)] = reach
        sums[pl.ds(32, 32)] = up
        sums[pl.ds(64, 32)] = down
        sums[pl.ds(96, 32)] = jnp.zeros((32, M), jnp.float32)

        @pl.loop(0, 4)
        def _(n):
            wide_dot(left, first, prod)
            sums[pl.ds(64, 64)] += prod[...]
            left[...] = prod[...].astype(half)
            wide_dot(left, second, prod)
            sums[pl.ds(0, 32)] += prod[pl.ds(0, 32)]

            @pl.when(n < 3)
            def _():
                sums[pl.ds(32, 32)] += prod[pl.ds(32, 32)]

            left[...] = prod[...].astype(half)

        out[...] = sums[...].astype(half)


def chain(where, keep, other, parts):
    return pl.pallas_call(
        chain_kernel,
        out_shape=[
            jax.ShapeDtypeStruct((128, M), jnp.bfloat16),
            jax.ShapeDtypeStruct((M, M), jnp.bfloat16),
            jax.ShapeDtypeStruct((M, M), jnp.bfloat16),
        ],
        in_specs=[SMEM] + [VMEM] * (2 + PARTS),
        out_specs=[VMEM] * 3,
        scratch_shapes=[
            pltpu.VMEM((64, M), jnp.bfloat16),
            pltpu.VMEM((64, M), jnp.float32),
            pltpu.VMEM((128, M), jnp.float32),
        ],
        compiler_params=pltpu.CompilerParams(vmem_limit_bytes=20 << 20),
        name="chain",
    )(where, keep, other, *parts)


def finish_kernel(last, where, lefts, keep, other, first, second, *refs):
    outs, prod = refs[:-1], refs[-1]

    @pl.when(where[0] == 0)
    def _():
        wide_dot(lefts.at[pl.ds(0, 64)], first, prod.at[0])
        wide_dot(lefts.at[pl.ds(64, 64)], second, prod.at[1])
        top = keep[0].astype(jnp.float32) + prod[1, pl.ds(32, 32)]
        up = prod[0, pl.ds(32, 32)]
        down = prod[1, pl.ds(0, 32)]
        bottom = other[1].astype(jnp.float32) + prod[0, pl.ds(0, 32)]
        if last:
            for at, block in enumerate((top, up, down, bottom)):
                outs[0][at] = block
            return
        mine, mine_half, rest_half = outs
        for odd, pair, rest in ((0, (top, down), (up, bottom)), (1, (up, bottom), (top, down))):

            @pl.when(where[3] == odd)
            def _(pair=pair, rest=rest):
                for at in range(2):
                    mine[at] = pair[at]
                    mine_half[at] = pair[at].astype(jnp.bfloat16)
                    rest_half[at] = rest[at].astype(jnp.bfloat16)


def finish(last, where, lefts, keep, other, first, second):
    pair = (2, 32, M)
    if last:
        shapes = [jax.ShapeDtypeStruct((4, 32, M), jnp.float32)]
    else:
        shapes = [
            jax.ShapeDtypeStruct(pair, kind) for kind in (jnp.float32, jnp.bfloat16, jnp.bfloat16)
        ]
    return pl.pallas_call(
        functools.partial(finish_kernel, last),
        out_shape=shapes,
        in_specs=[SMEM] + [VMEM] * 5,
        out_specs=[VMEM] * len(shapes),
        scratch_shapes=[pltpu.VMEM((2, 64, M), jnp.float32)],
        compiler_params=pltpu.CompilerParams(vmem_limit_bytes=16 << 20),
        name="finish",
    )(where, lefts, keep, other, first, second)


def star(last, where, keep, other):
    block = jnp.where(
        where[0] == 1,
        jnp.concatenate([keep[0], other[1]]),
        jnp.concatenate([other[0], keep[1]]),
    ).astype(jnp.bfloat16)
    parts_a, parts_b = gather(block)
    sums, first, second = chain(where, keep, other, parts_a + parts_b)
    lefts = send(sums, lambda x, c, y, z: (x, 0, y, z) if c == 1 else None)
    return finish(last, where, lefts, keep, other, first, second)


def body(ranges, pattern):
    slab = lax.axis_index("slab")
    panel = lax.axis_index("panel")
    core, odd = slab % NC, (slab // NC) % 2
    where = jnp.stack([core, panel // NZ, panel % NZ, odd]).astype(jnp.int32)

    keep, give = masked(where, pattern[0], ranges[0])
    other = send(give, lambda x, c, y, z: (x, 1 - c, y, z))
    mine, mine_half, rest_half = star(False, where, keep, other)

    near = send(rest_half, lambda x, c, y, z: (x, 1, y, z) if c == 0 else None)
    far = send(
        jnp.where(core == 0, mine_half, near), lambda x, c, y, z: (x ^ 1, c, y, z)
    ).astype(jnp.float32)
    local = jnp.where(core == 0, mine, near.astype(jnp.float32))
    swap = (odd == 1) == (core == 0)
    keep, other = jnp.where(swap, far, local), jnp.where(swap, local, far)
    (joint,) = star(True, where, keep, other)
    shared = send(joint, lambda x, c, y, z: (x, 1, y, z) if c == 0 else None)
    return jnp.where(core == 1, shared, joint)[None]


def solution(mesh):
    return jax.shard_map(
        body,
        mesh=mesh,
        in_specs=(P("slab", None, "panel", None), P("slab", None, None, None)),
        out_specs=P("slab", None, "panel", None),
        check_vma=False,
    )
```

```python
import functools
import jax
import jax.numpy as jnp
from jax import lax
from jax.experimental import pallas as pl
from jax.experimental.pallas import tpu as pltpu
from jax.sharding import PartitionSpec as P

M = 1024
BLK = 64
NX, NC, NY, NZ = 4, 2, 4, 8
AXES = ("slab", "panel")
PARTS = 8


def device(x, c, y, z):
    return ((x % NX) * NC + c) * NY * NZ + (y % NY) * NZ + z % NZ


def route(move):
    pairs = []
    for x in range(NX):
        for c in range(NC):
            for y in range(NY):
                for z in range(NZ):
                    target = move(x, c, y, z)
                    if target is not None:
                        pairs.append((device(x, c, y, z), device(*target)))
    return pairs


def send(block, move):
    return lax.ppermute(block, AXES, route(move))


def hop(axis, distance):
    def move(x, c, y, z):
        ahead = distance if c == 0 else -distance
        return (x, c, y + ahead, z) if axis == "y" else (x, c, y, z + ahead)

    return move


def gather(block):
    pair = send(block, hop("z", NZ // 2))
    wide_a = jnp.concatenate([block[:32], pair[:32]])
    wide_b = jnp.concatenate([block[32:], pair[32:]])
    ahead, behind = send(wide_a, hop("y", 1)), send(wide_a, hop("y", -1))
    wide_a = jnp.concatenate([wide_a, ahead, behind, send(wide_a, hop("y", 2))])
    ahead, behind = send(wide_b, hop("z", 1)), send(wide_b, hop("z", -1))
    wide_b = jnp.concatenate([wide_b, ahead, behind, send(ahead, hop("z", 1))])
    wide_a, wide_b = lax.optimization_barrier((wide_a, wide_b))
    parts = []
    for wide, axis in ((wide_a, "z"), (wide_b, "y")):
        ahead, wide = lax.optimization_barrier((send(wide, hop(axis, 1)), wide))
        parts.append([wide, ahead, send(wide, hop(axis, -1)), send(ahead, hop(axis, 1))])
    return parts


BACK = (0, 1, -1, 2)


def row_of(y, z):
    return pl.multiple_of((lax.rem(y + 2 * NY, NY) * NZ + lax.rem(z + 2 * NZ, NZ)) * 32, 32)


def order(where, parts, first, second):
    way, y, z = 1 - 2 * where[0], where[1], where[2]
    for part_a, part_b, outer in zip(parts[:4], parts[4:], BACK):
        for k, inner in enumerate(BACK):
            for j, far in enumerate((0, NZ // 2)):
                piece = pl.ds((2 * k + j) * 32, 32)
                at = pl.ds(row_of(y - way * inner, z - way * (outer + far)), 32)
                first[at] = part_a[piece]
                at = pl.ds(row_of(y - way * outer, z - way * (inner + far)), 32)
                second[at] = part_b[piece]


def wide_dot(left, factor, out):
    out[pl.ds(0, left.shape[0])] = jnp.dot(
        left[...], factor[...], preferred_element_type=jnp.float32
    )


def mask_kernel(where, pattern, ranges, keep, give):
    block_row = pl.ds(lax.div(where[1] * NZ + where[2], BLK // 32), 1)
    count = M // BLK
    spread = (
        lax.broadcasted_iota(jnp.int32, (count, M), 0)
        == lax.div(lax.broadcasted_iota(jnp.int32, (count, M), 1), BLK)
    ).astype(jnp.bfloat16)
    for b, (out, at) in enumerate(((keep, 0), (give, 0), (keep, 1), (give, 1))):
        present = pattern[b, block_row, :].astype(jnp.float32).astype(jnp.bfloat16)
        mask = jnp.dot(present, spread, preferred_element_type=jnp.float32)
        out[at] = ranges[b] * mask


VMEM = pl.BlockSpec(memory_space=pltpu.VMEM)
SMEM = pl.BlockSpec(memory_space=pltpu.SMEM)


def masked(where, pattern, ranges):
    return pl.pallas_call(
        mask_kernel,
        out_shape=[jax.ShapeDtypeStruct((2, 32, M), jnp.float32)] * 2,
        in_specs=[SMEM, VMEM, VMEM],
        out_specs=[VMEM, VMEM],
        compiler_params=pltpu.CompilerParams(vmem_limit_bytes=8 << 20),
        name="masked",
    )(where, pattern, ranges)


def chain_kernel(where, keep, other, *refs):
    parts, (out, first, second, left, prod, sums) = refs[:PARTS], refs[PARTS:]
    order(where, parts, first, second)

    @pl.when(where[0] == 1)
    def _():
        half = jnp.bfloat16
        down, up = keep[1].astype(jnp.float32), other[0].astype(jnp.float32)
        left[pl.ds(0, 32)] = down.astype(half)
        left[pl.ds(32, 32)] = up.astype(half)
        wide_dot(left, second, prod)
        reach = prod[pl.ds(0, 32)]
        left[pl.ds(0, 32)] = reach.astype(half)
        sums[pl.ds(0, 32)] = reach
        sums[pl.ds(32, 32)] = up
        sums[pl.ds(64, 32)] = down
        sums[pl.ds(96, 32)] = jnp.zeros((32, M), jnp.float32)

        @pl.loop(0, 4)
        def _(n):
            wide_dot(left, first, prod)
            sums[pl.ds(64, 64)] += prod[...]
            left[...] = prod[...].astype(half)
            wide_dot(left, second, prod)
            sums[pl.ds(0, 32)] += prod[pl.ds(0, 32)]

            @pl.when(n < 3)
            def _():
                sums[pl.ds(32, 32)] += prod[pl.ds(32, 32)]

            left[...] = prod[...].astype(half)

        out[...] = sums[...].astype(half)


def chain(where, keep, other, parts):
    return pl.pallas_call(
        chain_kernel,
        out_shape=[
            jax.ShapeDtypeStruct((128, M), jnp.bfloat16),
            jax.ShapeDtypeStruct((M, M), jnp.bfloat16),
            jax.ShapeDtypeStruct((M, M), jnp.bfloat16),
        ],
        in_specs=[SMEM] + [VMEM] * (2 + PARTS),
        out_specs=[VMEM] * 3,
        scratch_shapes=[
            pltpu.VMEM((64, M), jnp.bfloat16),
            pltpu.VMEM((64, M), jnp.float32),
            pltpu.VMEM((128, M), jnp.float32),
        ],
        compiler_params=pltpu.CompilerParams(vmem_limit_bytes=20 << 20),
        name="chain",
    )(where, keep, other, *parts)


def finish_kernel(last, where, lefts, keep, other, first, second, *refs):
    outs, prod = refs[:-1], refs[-1]

    @pl.when(where[0] == 0)
    def _():
        wide_dot(lefts.at[pl.ds(0, 64)], first, prod.at[0])
        wide_dot(lefts.at[pl.ds(64, 64)], second, prod.at[1])
        top = keep[0].astype(jnp.float32) + prod[1, pl.ds(32, 32)]
        up = prod[0, pl.ds(32, 32)]
        down = prod[1, pl.ds(0, 32)]
        bottom = other[1].astype(jnp.float32) + prod[0, pl.ds(0, 32)]
        if last:
            for at, block in enumerate((top, up, down, bottom)):
                outs[0][at] = block
            return
        mine, mine_half, rest_half = outs
        for odd, pair, rest in ((0, (top, down), (up, bottom)), (1, (up, bottom), (top, down))):

            @pl.when(where[3] == odd)
            def _(pair=pair, rest=rest):
                for at in range(2):
                    mine[at] = pair[at]
                    mine_half[at] = pair[at].astype(jnp.bfloat16)
                    rest_half[at] = rest[at].astype(jnp.bfloat16)


def finish(last, where, lefts, keep, other, first, second):
    pair = (2, 32, M)
    if last:
        shapes = [jax.ShapeDtypeStruct((4, 32, M), jnp.float32)]
    else:
        shapes = [
            jax.ShapeDtypeStruct(pair, kind) for kind in (jnp.float32, jnp.bfloat16, jnp.bfloat16)
        ]
    return pl.pallas_call(
        functools.partial(finish_kernel, last),
        out_shape=shapes,
        in_specs=[SMEM] + [VMEM] * 5,
        out_specs=[VMEM] * len(shapes),
        scratch_shapes=[pltpu.VMEM((2, 64, M), jnp.float32)],
        compiler_params=pltpu.CompilerParams(vmem_limit_bytes=16 << 20),
        name="finish",
    )(where, lefts, keep, other, first, second)


def star(last, where, keep, other):
    block = jnp.where(
        where[0] == 1,
        jnp.concatenate([keep[0], other[1]]),
        jnp.concatenate([other[0], keep[1]]),
    ).astype(jnp.bfloat16)
    parts_a, parts_b = gather(block)
    sums, first, second = chain(where, keep, other, parts_a + parts_b)
    lefts = send(sums, lambda x, c, y, z: (x, 0, y, z) if c == 1 else None)
    return finish(last, where, lefts, keep, other, first, second)


def body(ranges, pattern):
    slab = lax.axis_index("slab")
    panel = lax.axis_index("panel")
    core, odd = slab % NC, (slab // NC) % 2
    where = jnp.stack([core, panel // NZ, panel % NZ, odd]).astype(jnp.int32)

    keep, give = masked(where, pattern[0], ranges[0])
    other = send(give, lambda x, c, y, z: (x, 1 - c, y, z))
    mine, mine_half, rest_half = star(False, where, keep, other)

    near = send(rest_half, lambda x, c, y, z: (x, 1, y, z) if c == 0 else None)
    far = send(
        jnp.where(core == 0, mine_half, near), lambda x, c, y, z: (x ^ 1, c, y, z)
    ).astype(jnp.float32)
    local = jnp.where(core == 0, mine, near.astype(jnp.float32))
    swap = (odd == 1) == (core == 0)
    keep, other = jnp.where(swap, far, local), jnp.where(swap, local, far)
    (joint,) = star(True, where, keep, other)
    shared = send(joint, lambda x, c, y, z: (x, 1, y, z) if c == 0 else None)
    return jnp.where(core == 1, shared, joint)[None]


def solution(mesh):
    return jax.shard_map(
        body,
        mesh=mesh,
        in_specs=(P("slab", None, "panel", None), P("slab", None, None, None)),
        out_specs=P("slab", None, "panel", None),
        check_vma=False,
    )
```

```python
import functools
import jax
import jax.numpy as jnp
from jax import lax
from jax.experimental import pallas as pl
from jax.experimental.pallas import tpu as pltpu
from jax.sharding import PartitionSpec as P

M = 1024
BLK = 64
NX, NC, NY, NZ = 4, 2, 4, 8
AXES = ("slab", "panel")
PARTS = 8


def device(x, c, y, z):
    return ((x % NX) * NC + c) * NY * NZ + (y % NY) * NZ + z % NZ


def route(move):
    pairs = []
    for x in range(NX):
        for c in range(NC):
            for y in range(NY):
                for z in range(NZ):
                    target = move(x, c, y, z)
                    if target is not None:
                        pairs.append((device(x, c, y, z), device(*target)))
    return pairs


def send(block, move):
    return lax.ppermute(block, AXES, route(move))


def hop(axis, distance):
    def move(x, c, y, z):
        ahead = distance if c == 0 else -distance
        return (x, c, y + ahead, z) if axis == "y" else (x, c, y, z + ahead)

    return move


def gather(block):
    pair = send(block, hop("z", NZ // 2))
    wide_a = jnp.concatenate([block[:32], pair[:32]])
    wide_b = jnp.concatenate([block[32:], pair[32:]])
    ahead, behind = send(wide_a, hop("y", 1)), send(wide_a, hop("y", -1))
    wide_a = jnp.concatenate([wide_a, ahead, behind, send(wide_a, hop("y", 2))])
    ahead, behind = send(wide_b, hop("z", 1)), send(wide_b, hop("z", -1))
    wide_b = jnp.concatenate([wide_b, ahead, behind, send(ahead, hop("z", 1))])
    wide_a, wide_b = lax.optimization_barrier((wide_a, wide_b))
    parts = []
    for wide, axis in ((wide_a, "z"), (wide_b, "y")):
        ahead, behind = send(wide, hop(axis, 1)), send(wide, hop(axis, -1))
        parts.append([wide, ahead, behind, send(ahead, hop(axis, 1))])
    return parts


BACK = (0, 1, -1, 2)


def row_of(y, z):
    return pl.multiple_of((lax.rem(y + 2 * NY, NY) * NZ + lax.rem(z + 2 * NZ, NZ)) * 32, 32)


def order(where, parts, first, second):
    way, y, z = 1 - 2 * where[0], where[1], where[2]
    for part_a, part_b, outer in zip(parts[:4], parts[4:], BACK):
        for k, inner in enumerate(BACK):
            for j, far in enumerate((0, NZ // 2)):
                piece = pl.ds((2 * k + j) * 32, 32)
                at = pl.ds(row_of(y - way * inner, z - way * (outer + far)), 32)
                first[at] = part_a[piece]
                at = pl.ds(row_of(y - way * outer, z - way * (inner + far)), 32)
                second[at] = part_b[piece]


def wide_dot(left, factor, out):
    out[pl.ds(0, left.shape[0])] = jnp.dot(
        left[...], factor[...], preferred_element_type=jnp.float32
    )


def mask_kernel(where, pattern, ranges, keep, give):
    block_row = pl.ds(lax.div(where[1] * NZ + where[2], BLK // 32), 1)
    count = M // BLK
    spread = (
        lax.broadcasted_iota(jnp.int32, (count, M), 0)
        == lax.div(lax.broadcasted_iota(jnp.int32, (count, M), 1), BLK)
    ).astype(jnp.bfloat16)
    for b, (out, at) in enumerate(((keep, 0), (give, 0), (keep, 1), (give, 1))):
        present = pattern[b, block_row, :].astype(jnp.float32).astype(jnp.bfloat16)
        mask = jnp.dot(present, spread, preferred_element_type=jnp.float32)
        out[at] = ranges[b] * mask


VMEM = pl.BlockSpec(memory_space=pltpu.VMEM)
SMEM = pl.BlockSpec(memory_space=pltpu.SMEM)


def masked(where, pattern, ranges):
    return pl.pallas_call(
        mask_kernel,
        out_shape=[jax.ShapeDtypeStruct((2, 32, M), jnp.float32)] * 2,
        in_specs=[SMEM, VMEM, VMEM],
        out_specs=[VMEM, VMEM],
        compiler_params=pltpu.CompilerParams(vmem_limit_bytes=8 << 20),
        name="masked",
    )(where, pattern, ranges)


def chain_kernel(where, keep, other, *refs):
    parts, (out, first, second, left, prod, sums) = refs[:PARTS], refs[PARTS:]
    order(where, parts, first, second)

    @pl.when(where[0] == 1)
    def _():
        half = jnp.bfloat16
        down, up = keep[1].astype(jnp.float32), other[0].astype(jnp.float32)
        left[pl.ds(0, 32)] = down.astype(half)
        left[pl.ds(32, 32)] = up.astype(half)
        wide_dot(left, second, prod)
        reach = prod[pl.ds(0, 32)]
        left[pl.ds(0, 32)] = reach.astype(half)
        sums[pl.ds(0, 32)] = reach
        sums[pl.ds(32, 32)] = up
        sums[pl.ds(64, 32)] = down
        sums[pl.ds(96, 32)] = jnp.zeros((32, M), jnp.float32)

        @pl.loop(0, 4)
        def _(n):
            wide_dot(left, first, prod)
            sums[pl.ds(64, 64)] += prod[...]
            left[...] = prod[...].astype(half)
            wide_dot(left, second, prod)
            sums[pl.ds(0, 32)] += prod[pl.ds(0, 32)]

            @pl.when(n < 3)
            def _():
                sums[pl.ds(32, 32)] += prod[pl.ds(32, 32)]

            left[...] = prod[...].astype(half)

        out[...] = sums[...].astype(half)


def chain(where, keep, other, parts):
    return pl.pallas_call(
        chain_kernel,
        out_shape=[
            jax.ShapeDtypeStruct((128, M), jnp.bfloat16),
            jax.ShapeDtypeStruct((M, M), jnp.bfloat16),
            jax.ShapeDtypeStruct((M, M), jnp.bfloat16),
        ],
        in_specs=[SMEM] + [VMEM] * (2 + PARTS),
        out_specs=[VMEM] * 3,
        scratch_shapes=[
            pltpu.VMEM((64, M), jnp.bfloat16),
            pltpu.VMEM((64, M), jnp.float32),
            pltpu.VMEM((128, M), jnp.float32),
        ],
        compiler_params=pltpu.CompilerParams(vmem_limit_bytes=20 << 20),
        name="chain",
    )(where, keep, other, *parts)


def finish_kernel(last, where, lefts, keep, other, first, second, *refs):
    outs, prod = refs[:-1], refs[-1]

    @pl.when(where[0] == 0)
    def _():
        wide_dot(lefts.at[pl.ds(0, 64)], first, prod.at[0])
        wide_dot(lefts.at[pl.ds(64, 64)], second, prod.at[1])
        top = keep[0].astype(jnp.float32) + prod[1, pl.ds(32, 32)]
        up = prod[0, pl.ds(32, 32)]
        down = prod[1, pl.ds(0, 32)]
        bottom = other[1].astype(jnp.float32) + prod[0, pl.ds(0, 32)]
        if last:
            for at, block in enumerate((top, up, down, bottom)):
                outs[0][at] = block
            return
        mine, mine_half, rest_half = outs
        for odd, pair, rest in ((0, (top, down), (up, bottom)), (1, (up, bottom), (top, down))):

            @pl.when(where[3] == odd)
            def _(pair=pair, rest=rest):
                for at in range(2):
                    mine[at] = pair[at]
                    mine_half[at] = pair[at].astype(jnp.bfloat16)
                    rest_half[at] = rest[at].astype(jnp.bfloat16)


def finish(last, where, lefts, keep, other, first, second):
    pair = (2, 32, M)
    if last:
        shapes = [jax.ShapeDtypeStruct((4, 32, M), jnp.float32)]
    else:
        shapes = [
            jax.ShapeDtypeStruct(pair, kind) for kind in (jnp.float32, jnp.bfloat16, jnp.bfloat16)
        ]
    return pl.pallas_call(
        functools.partial(finish_kernel, last),
        out_shape=shapes,
        in_specs=[SMEM] + [VMEM] * 5,
        out_specs=[VMEM] * len(shapes),
        scratch_shapes=[pltpu.VMEM((2, 64, M), jnp.float32)],
        compiler_params=pltpu.CompilerParams(vmem_limit_bytes=16 << 20),
        name="finish",
    )(where, lefts, keep, other, first, second)


def star(last, where, keep, other):
    block = jnp.where(
        where[0] == 1,
        jnp.concatenate([keep[0], other[1]]),
        jnp.concatenate([other[0], keep[1]]),
    ).astype(jnp.bfloat16)
    parts_a, parts_b = gather(block)
    sums, first, second = chain(where, keep, other, parts_a + parts_b)
    lefts = send(sums, lambda x, c, y, z: (x, 0, y, z) if c == 1 else None)
    return finish(last, where, lefts, keep, other, first, second)


def body(ranges, pattern):
    slab = lax.axis_index("slab")
    panel = lax.axis_index("panel")
    core, odd = slab % NC, (slab // NC) % 2
    where = jnp.stack([core, panel // NZ, panel % NZ, odd]).astype(jnp.int32)

    keep, give = masked(where, pattern[0], ranges[0])
    other = send(give, lambda x, c, y, z: (x, 1 - c, y, z))
    mine, mine_half, rest_half = star(False, where, keep, other)

    near = send(rest_half, lambda x, c, y, z: (x, 1, y, z) if c == 0 else None)
    far = send(
        jnp.where(core == 0, mine_half, near), lambda x, c, y, z: (x ^ 1, c, y, z)
    ).astype(jnp.float32)
    local = jnp.where(core == 0, mine, near.astype(jnp.float32))
    swap = (odd == 1) == (core == 0)
    keep, other = jnp.where(swap, far, local), jnp.where(swap, local, far)
    (joint,) = star(True, where, keep, other)
    shared = send(joint, lambda x, c, y, z: (x, 1, y, z) if c == 0 else None)
    return jnp.where(core == 1, shared, joint)[None]


def solution(mesh):
    return jax.shard_map(
        body,
        mesh=mesh,
        in_specs=(P("slab", None, "panel", None), P("slab", None, None, None)),
        out_specs=P("slab", None, "panel", None),
        check_vma=False,
    )
```

```python
import functools
import jax
import jax.numpy as jnp
from jax import lax
from jax.experimental import pallas as pl
from jax.experimental.pallas import tpu as pltpu
from jax.sharding import PartitionSpec as P

M = 1024
BLK = 64
NX, NC, NY, NZ = 4, 2, 4, 8
AXES = ("slab", "panel")
PARTS = 8


def device(x, c, y, z):
    return ((x % NX) * NC + c) * NY * NZ + (y % NY) * NZ + z % NZ


def route(move):
    pairs = []
    for x in range(NX):
        for c in range(NC):
            for y in range(NY):
                for z in range(NZ):
                    target = move(x, c, y, z)
                    if target is not None:
                        pairs.append((device(x, c, y, z), device(*target)))
    return pairs


def send(block, move):
    return lax.ppermute(block, AXES, route(move))


def hop(axis, distance):
    def move(x, c, y, z):
        ahead = distance if c == 0 else -distance
        return (x, c, y + ahead, z) if axis == "y" else (x, c, y, z + ahead)

    return move


def gather(block):
    wide_a, wide_b = block[:32], block[32:]
    wide_a = jnp.concatenate([wide_a, send(wide_a, hop("z", NZ // 2))])
    wide_b = jnp.concatenate([wide_b, send(wide_b, hop("z", NZ // 2))])
    ahead, behind = send(wide_a, hop("y", 1)), send(wide_a, hop("y", -1))
    wide_a = jnp.concatenate([wide_a, ahead, behind, send(wide_a, hop("y", 2))])
    ahead, behind = send(wide_b, hop("z", 1)), send(wide_b, hop("z", -1))
    wide_b = jnp.concatenate([wide_b, ahead, behind, send(ahead, hop("z", 1))])
    wide_a, wide_b = lax.optimization_barrier((wide_a, wide_b))
    parts = []
    for wide, axis in ((wide_a, "z"), (wide_b, "y")):
        ahead, behind = send(wide, hop(axis, 1)), send(wide, hop(axis, -1))
        parts.append([wide, ahead, behind, send(ahead, hop(axis, 1))])
    return parts


BACK = (0, 1, -1, 2)


def row_of(y, z):
    return pl.multiple_of((lax.rem(y + 2 * NY, NY) * NZ + lax.rem(z + 2 * NZ, NZ)) * 32, 32)


def order(where, parts, first, second):
    way, y, z = 1 - 2 * where[0], where[1], where[2]
    for part_a, part_b, outer in zip(parts[:4], parts[4:], BACK):
        for k, inner in enumerate(BACK):
            for j, far in enumerate((0, NZ // 2)):
                piece = pl.ds((2 * k + j) * 32, 32)
                at = pl.ds(row_of(y - way * inner, z - way * (outer + far)), 32)
                first[at] = part_a[piece]
                at = pl.ds(row_of(y - way * outer, z - way * (inner + far)), 32)
                second[at] = part_b[piece]


def wide_dot(left, factor, out):
    out[pl.ds(0, left.shape[0])] = jnp.dot(
        left[...], factor[...], preferred_element_type=jnp.float32
    )


def mask_kernel(where, pattern, ranges, keep, give):
    block_row = pl.ds(lax.div(where[1] * NZ + where[2], BLK // 32), 1)
    count = M // BLK
    spread = (
        lax.broadcasted_iota(jnp.int32, (count, M), 0)
        == lax.div(lax.broadcasted_iota(jnp.int32, (count, M), 1), BLK)
    ).astype(jnp.bfloat16)
    for b, (out, at) in enumerate(((keep, 0), (give, 0), (keep, 1), (give, 1))):
        present = pattern[b, block_row, :].astype(jnp.float32).astype(jnp.bfloat16)
        mask = jnp.dot(present, spread, preferred_element_type=jnp.float32)
        out[at] = ranges[b] * mask


VMEM = pl.BlockSpec(memory_space=pltpu.VMEM)
SMEM = pl.BlockSpec(memory_space=pltpu.SMEM)


def masked(where, pattern, ranges):
    return pl.pallas_call(
        mask_kernel,
        out_shape=[jax.ShapeDtypeStruct((2, 32, M), jnp.float32)] * 2,
        in_specs=[SMEM, VMEM, VMEM],
        out_specs=[VMEM, VMEM],
        compiler_params=pltpu.CompilerParams(vmem_limit_bytes=8 << 20),
        name="masked",
    )(where, pattern, ranges)


def chain_kernel(where, keep, other, *refs):
    parts, (out, first, second, left, prod, sums) = refs[:PARTS], refs[PARTS:]
    order(where, parts, first, second)

    @pl.when(where[0] == 1)
    def _():
        half = jnp.bfloat16
        down, up = keep[1].astype(jnp.float32), other[0].astype(jnp.float32)
        left[pl.ds(0, 32)] = down.astype(half)
        left[pl.ds(32, 32)] = up.astype(half)
        wide_dot(left, second, prod)
        reach = prod[pl.ds(0, 32)]
        left[pl.ds(0, 32)] = reach.astype(half)
        sums[pl.ds(0, 32)] = reach
        sums[pl.ds(32, 32)] = up
        sums[pl.ds(64, 32)] = down
        sums[pl.ds(96, 32)] = jnp.zeros((32, M), jnp.float32)

        @pl.loop(0, 4)
        def _(n):
            wide_dot(left, first, prod)
            sums[pl.ds(64, 64)] += prod[...]
            left[...] = prod[...].astype(half)
            wide_dot(left, second, prod)
            sums[pl.ds(0, 32)] += prod[pl.ds(0, 32)]

            @pl.when(n < 3)
            def _():
                sums[pl.ds(32, 32)] += prod[pl.ds(32, 32)]

            left[...] = prod[...].astype(half)

        out[...] = sums[...].astype(half)


def chain(where, keep, other, parts):
    return pl.pallas_call(
        chain_kernel,
        out_shape=[
            jax.ShapeDtypeStruct((128, M), jnp.bfloat16),
            jax.ShapeDtypeStruct((M, M), jnp.bfloat16),
            jax.ShapeDtypeStruct((M, M), jnp.bfloat16),
        ],
        in_specs=[SMEM] + [VMEM] * (2 + PARTS),
        out_specs=[VMEM] * 3,
        scratch_shapes=[
            pltpu.VMEM((64, M), jnp.bfloat16),
            pltpu.VMEM((64, M), jnp.float32),
            pltpu.VMEM((128, M), jnp.float32),
        ],
        compiler_params=pltpu.CompilerParams(vmem_limit_bytes=20 << 20),
        name="chain",
    )(where, keep, other, *parts)


def finish_kernel(last, where, lefts, keep, other, first, second, *refs):
    outs, prod = refs[:-1], refs[-1]

    @pl.when(where[0] == 0)
    def _():
        wide_dot(lefts.at[pl.ds(0, 64)], first, prod.at[0])
        wide_dot(lefts.at[pl.ds(64, 64)], second, prod.at[1])
        top = keep[0].astype(jnp.float32) + prod[1, pl.ds(32, 32)]
        up = prod[0, pl.ds(32, 32)]
        down = prod[1, pl.ds(0, 32)]
        bottom = other[1].astype(jnp.float32) + prod[0, pl.ds(0, 32)]
        if last:
            for at, block in enumerate((top, up, down, bottom)):
                outs[0][at] = block
            return
        mine, mine_half, rest_half = outs
        for odd, pair, rest in ((0, (top, down), (up, bottom)), (1, (up, bottom), (top, down))):

            @pl.when(where[3] == odd)
            def _(pair=pair, rest=rest):
                for at in range(2):
                    mine[at] = pair[at]
                    mine_half[at] = pair[at].astype(jnp.bfloat16)
                    rest_half[at] = rest[at].astype(jnp.bfloat16)


def finish(last, where, lefts, keep, other, first, second):
    pair = (2, 32, M)
    if last:
        shapes = [jax.ShapeDtypeStruct((4, 32, M), jnp.float32)]
    else:
        shapes = [
            jax.ShapeDtypeStruct(pair, kind) for kind in (jnp.float32, jnp.bfloat16, jnp.bfloat16)
        ]
    return pl.pallas_call(
        functools.partial(finish_kernel, last),
        out_shape=shapes,
        in_specs=[SMEM] + [VMEM] * 5,
        out_specs=[VMEM] * len(shapes),
        scratch_shapes=[pltpu.VMEM((2, 64, M), jnp.float32)],
        compiler_params=pltpu.CompilerParams(vmem_limit_bytes=16 << 20),
        name="finish",
    )(where, lefts, keep, other, first, second)


def star(last, where, keep, other):
    block = jnp.where(
        where[0] == 1,
        jnp.concatenate([keep[0], other[1]]),
        jnp.concatenate([other[0], keep[1]]),
    ).astype(jnp.bfloat16)
    parts_a, parts_b = gather(block)
    sums, first, second = chain(where, keep, other, parts_a + parts_b)
    lefts = send(sums, lambda x, c, y, z: (x, 0, y, z) if c == 1 else None)
    return finish(last, where, lefts, keep, other, first, second)


def body(ranges, pattern):
    slab = lax.axis_index("slab")
    panel = lax.axis_index("panel")
    core, odd = slab % NC, (slab // NC) % 2
    where = jnp.stack([core, panel // NZ, panel % NZ, odd]).astype(jnp.int32)

    keep, give = masked(where, pattern[0], ranges[0])
    other = send(give, lambda x, c, y, z: (x, 1 - c, y, z))
    mine, mine_half, rest_half = star(False, where, keep, other)

    near = send(rest_half, lambda x, c, y, z: (x, 1, y, z) if c == 0 else None)
    far = send(
        jnp.where(core == 0, mine_half, near), lambda x, c, y, z: (x ^ 1, c, y, z)
    ).astype(jnp.float32)
    local = jnp.where(core == 0, mine, near.astype(jnp.float32))
    swap = (odd == 1) == (core == 0)
    keep, other = jnp.where(swap, far, local), jnp.where(swap, local, far)
    (joint,) = star(True, where, keep, other)
    shared = send(joint, lambda x, c, y, z: (x, 1, y, z) if c == 0 else None)
    return jnp.where(core == 1, shared, joint)[None]


def solution(mesh):
    return jax.shard_map(
        body,
        mesh=mesh,
        in_specs=(P("slab", None, "panel", None), P("slab", None, None, None)),
        out_specs=P("slab", None, "panel", None),
        check_vma=False,
    )
```

```python
import functools
import jax
import jax.numpy as jnp
from jax import lax
from jax.experimental import pallas as pl
from jax.experimental.pallas import tpu as pltpu
from jax.sharding import PartitionSpec as P

M = 1024
BLK = 64
NX, NC, NY, NZ = 4, 2, 4, 8
AXES = ("slab", "panel")
PARTS = 8


def device(x, c, y, z):
    return ((x % NX) * NC + c) * NY * NZ + (y % NY) * NZ + z % NZ


def route(move):
    pairs = []
    for x in range(NX):
        for c in range(NC):
            for y in range(NY):
                for z in range(NZ):
                    target = move(x, c, y, z)
                    if target is not None:
                        pairs.append((device(x, c, y, z), device(*target)))
    return pairs


def send(block, move):
    return lax.ppermute(block, AXES, route(move))


def hop(axis, distance):
    def move(x, c, y, z):
        ahead = distance if c == 0 else -distance
        return (x, c, y + ahead, z) if axis == "y" else (x, c, y, z + ahead)

    return move


def gather(block):
    wide_a, wide_b = block[:32], block[32:]
    wide_a = jnp.concatenate([wide_a, send(wide_a, hop("z", NZ // 2))])
    wide_b = jnp.concatenate([wide_b, send(wide_b, hop("z", NZ // 2))])
    ahead, behind = send(wide_a, hop("y", 1)), send(wide_a, hop("y", -1))
    wide_a = jnp.concatenate([wide_a, ahead, behind, send(wide_a, hop("y", 2))])
    ahead, wide_b = lax.optimization_barrier((send(wide_b, hop("z", 1)), wide_b))
    behind = send(wide_b, hop("z", -1))
    wide_b = jnp.concatenate([wide_b, ahead, behind, send(ahead, hop("z", 1))])
    wide_a, wide_b = lax.optimization_barrier((wide_a, wide_b))
    parts = []
    for wide, axis in ((wide_a, "z"), (wide_b, "y")):
        ahead, behind = send(wide, hop(axis, 1)), send(wide, hop(axis, -1))
        parts.append([wide, ahead, behind, send(ahead, hop(axis, 1))])
    return parts


BACK = (0, 1, -1, 2)


def row_of(y, z):
    return pl.multiple_of((lax.rem(y + 2 * NY, NY) * NZ + lax.rem(z + 2 * NZ, NZ)) * 32, 32)


def order(where, parts, first, second):
    way, y, z = 1 - 2 * where[0], where[1], where[2]
    for part_a, part_b, outer in zip(parts[:4], parts[4:], BACK):
        for k, inner in enumerate(BACK):
            for j, far in enumerate((0, NZ // 2)):
                piece = pl.ds((2 * k + j) * 32, 32)
                at = pl.ds(row_of(y - way * inner, z - way * (outer + far)), 32)
                first[at] = part_a[piece]
                at = pl.ds(row_of(y - way * outer, z - way * (inner + far)), 32)
                second[at] = part_b[piece]


def wide_dot(left, factor, out):
    out[pl.ds(0, left.shape[0])] = jnp.dot(
        left[...], factor[...], preferred_element_type=jnp.float32
    )


def mask_kernel(where, pattern, ranges, keep, give):
    block_row = pl.ds(lax.div(where[1] * NZ + where[2], BLK // 32), 1)
    count = M // BLK
    spread = (
        lax.broadcasted_iota(jnp.int32, (count, M), 0)
        == lax.div(lax.broadcasted_iota(jnp.int32, (count, M), 1), BLK)
    ).astype(jnp.bfloat16)
    for b, (out, at) in enumerate(((keep, 0), (give, 0), (keep, 1), (give, 1))):
        present = pattern[b, block_row, :].astype(jnp.float32).astype(jnp.bfloat16)
        mask = jnp.dot(present, spread, preferred_element_type=jnp.float32)
        out[at] = ranges[b] * mask


VMEM = pl.BlockSpec(memory_space=pltpu.VMEM)
SMEM = pl.BlockSpec(memory_space=pltpu.SMEM)


def masked(where, pattern, ranges):
    return pl.pallas_call(
        mask_kernel,
        out_shape=[jax.ShapeDtypeStruct((2, 32, M), jnp.float32)] * 2,
        in_specs=[SMEM, VMEM, VMEM],
        out_specs=[VMEM, VMEM],
        compiler_params=pltpu.CompilerParams(vmem_limit_bytes=8 << 20),
        name="masked",
    )(where, pattern, ranges)


def chain_kernel(where, keep, other, *refs):
    parts, (out, first, second, left, prod, sums) = refs[:PARTS], refs[PARTS:]
    order(where, parts, first, second)

    @pl.when(where[0] == 1)
    def _():
        half = jnp.bfloat16
        down, up = keep[1].astype(jnp.float32), other[0].astype(jnp.float32)
        left[pl.ds(0, 32)] = down.astype(half)
        left[pl.ds(32, 32)] = up.astype(half)
        wide_dot(left, second, prod)
        reach = prod[pl.ds(0, 32)]
        left[pl.ds(0, 32)] = reach.astype(half)
        sums[pl.ds(0, 32)] = reach
        sums[pl.ds(32, 32)] = up
        sums[pl.ds(64, 32)] = down
        sums[pl.ds(96, 32)] = jnp.zeros((32, M), jnp.float32)

        @pl.loop(0, 4)
        def _(n):
            wide_dot(left, first, prod)
            sums[pl.ds(64, 64)] += prod[...]
            left[...] = prod[...].astype(half)
            wide_dot(left, second, prod)
            sums[pl.ds(0, 32)] += prod[pl.ds(0, 32)]

            @pl.when(n < 3)
            def _():
                sums[pl.ds(32, 32)] += prod[pl.ds(32, 32)]

            left[...] = prod[...].astype(half)

        out[...] = sums[...].astype(half)


def chain(where, keep, other, parts):
    return pl.pallas_call(
        chain_kernel,
        out_shape=[
            jax.ShapeDtypeStruct((128, M), jnp.bfloat16),
            jax.ShapeDtypeStruct((M, M), jnp.bfloat16),
            jax.ShapeDtypeStruct((M, M), jnp.bfloat16),
        ],
        in_specs=[SMEM] + [VMEM] * (2 + PARTS),
        out_specs=[VMEM] * 3,
        scratch_shapes=[
            pltpu.VMEM((64, M), jnp.bfloat16),
            pltpu.VMEM((64, M), jnp.float32),
            pltpu.VMEM((128, M), jnp.float32),
        ],
        compiler_params=pltpu.CompilerParams(vmem_limit_bytes=20 << 20),
        name="chain",
    )(where, keep, other, *parts)


def finish_kernel(last, where, lefts, keep, other, first, second, *refs):
    outs, prod = refs[:-1], refs[-1]

    @pl.when(where[0] == 0)
    def _():
        wide_dot(lefts.at[pl.ds(0, 64)], first, prod.at[0])
        wide_dot(lefts.at[pl.ds(64, 64)], second, prod.at[1])
        top = keep[0].astype(jnp.float32) + prod[1, pl.ds(32, 32)]
        up = prod[0, pl.ds(32, 32)]
        down = prod[1, pl.ds(0, 32)]
        bottom = other[1].astype(jnp.float32) + prod[0, pl.ds(0, 32)]
        if last:
            for at, block in enumerate((top, up, down, bottom)):
                outs[0][at] = block
            return
        mine, mine_half, rest_half = outs
        for odd, pair, rest in ((0, (top, down), (up, bottom)), (1, (up, bottom), (top, down))):

            @pl.when(where[3] == odd)
            def _(pair=pair, rest=rest):
                for at in range(2):
                    mine[at] = pair[at]
                    mine_half[at] = pair[at].astype(jnp.bfloat16)
                    rest_half[at] = rest[at].astype(jnp.bfloat16)


def finish(last, where, lefts, keep, other, first, second):
    pair = (2, 32, M)
    if last:
        shapes = [jax.ShapeDtypeStruct((4, 32, M), jnp.float32)]
    else:
        shapes = [
            jax.ShapeDtypeStruct(pair, kind) for kind in (jnp.float32, jnp.bfloat16, jnp.bfloat16)
        ]
    return pl.pallas_call(
        functools.partial(finish_kernel, last),
        out_shape=shapes,
        in_specs=[SMEM] + [VMEM] * 5,
        out_specs=[VMEM] * len(shapes),
        scratch_shapes=[pltpu.VMEM((2, 64, M), jnp.float32)],
        compiler_params=pltpu.CompilerParams(vmem_limit_bytes=16 << 20),
        name="finish",
    )(where, lefts, keep, other, first, second)


def star(last, where, keep, other):
    block = jnp.where(
        where[0] == 1,
        jnp.concatenate([keep[0], other[1]]),
        jnp.concatenate([other[0], keep[1]]),
    ).astype(jnp.bfloat16)
    parts_a, parts_b = gather(block)
    sums, first, second = chain(where, keep, other, parts_a + parts_b)
    lefts = send(sums, lambda x, c, y, z: (x, 0, y, z) if c == 1 else None)
    return finish(last, where, lefts, keep, other, first, second)


def body(ranges, pattern):
    slab = lax.axis_index("slab")
    panel = lax.axis_index("panel")
    core, odd = slab % NC, (slab // NC) % 2
    where = jnp.stack([core, panel // NZ, panel % NZ, odd]).astype(jnp.int32)

    keep, give = masked(where, pattern[0], ranges[0])
    other = send(give, lambda x, c, y, z: (x, 1 - c, y, z))
    mine, mine_half, rest_half = star(False, where, keep, other)

    near = send(rest_half, lambda x, c, y, z: (x, 1, y, z) if c == 0 else None)
    far = send(
        jnp.where(core == 0, mine_half, near), lambda x, c, y, z: (x ^ 1, c, y, z)
    ).astype(jnp.float32)
    local = jnp.where(core == 0, mine, near.astype(jnp.float32))
    swap = (odd == 1) == (core == 0)
    keep, other = jnp.where(swap, far, local), jnp.where(swap, local, far)
    (joint,) = star(True, where, keep, other)
    shared = send(joint, lambda x, c, y, z: (x, 1, y, z) if c == 0 else None)
    return jnp.where(core == 1, shared, joint)[None]


def solution(mesh):
    return jax.shard_map(
        body,
        mesh=mesh,
        in_specs=(P("slab", None, "panel", None), P("slab", None, None, None)),
        out_specs=P("slab", None, "panel", None),
        check_vma=False,
    )
```

```python
import functools
import jax
import jax.numpy as jnp
from jax import lax
from jax.experimental import pallas as pl
from jax.experimental.pallas import tpu as pltpu
from jax.sharding import PartitionSpec as P

M = 1024
BLK = 64
NX, NC, NY, NZ = 4, 2, 4, 8
AXES = ("slab", "panel")
PARTS = 8


def device(x, c, y, z):
    return ((x % NX) * NC + c) * NY * NZ + (y % NY) * NZ + z % NZ


def route(move):
    pairs = []
    for x in range(NX):
        for c in range(NC):
            for y in range(NY):
                for z in range(NZ):
                    target = move(x, c, y, z)
                    if target is not None:
                        pairs.append((device(x, c, y, z), device(*target)))
    return pairs


def send(block, move):
    return lax.ppermute(block, AXES, route(move))


def hop(axis, distance):
    def move(x, c, y, z):
        ahead = distance if c == 0 else -distance
        return (x, c, y + ahead, z) if axis == "y" else (x, c, y, z + ahead)

    return move


def gather(block):
    wide_a, wide_b = block[:32], block[32:]
    wide_a = jnp.concatenate([wide_a, send(wide_a, hop("z", NZ // 2))])
    wide_b = jnp.concatenate([wide_b, send(wide_b, hop("z", NZ // 2))])
    ahead, behind = send(wide_a, hop("y", 1)), send(wide_a, hop("y", -1))
    wide_a = jnp.concatenate([wide_a, ahead, behind, send(wide_a, hop("y", 2))])
    wide_b = jnp.concatenate([wide_b] + [send(wide_b, hop("z", d)) for d in BACK[1:]])
    wide_a, wide_b = lax.optimization_barrier((wide_a, wide_b))
    parts = []
    for wide, axis in ((wide_a, "z"), (wide_b, "y")):
        ahead, behind = send(wide, hop(axis, 1)), send(wide, hop(axis, -1))
        parts.append([wide, ahead, behind, send(ahead, hop(axis, 1))])
    return parts


BACK = (0, 1, -1, 2)


def row_of(y, z):
    return pl.multiple_of((lax.rem(y + 2 * NY, NY) * NZ + lax.rem(z + 2 * NZ, NZ)) * 32, 32)


def order(where, parts, first, second):
    way, y, z = 1 - 2 * where[0], where[1], where[2]
    for part_a, part_b, outer in zip(parts[:4], parts[4:], BACK):
        for k, inner in enumerate(BACK):
            for j, far in enumerate((0, NZ // 2)):
                piece = pl.ds((2 * k + j) * 32, 32)
                at = pl.ds(row_of(y - way * inner, z - way * (outer + far)), 32)
                first[at] = part_a[piece]
                at = pl.ds(row_of(y - way * outer, z - way * (inner + far)), 32)
                second[at] = part_b[piece]


def wide_dot(left, factor, out):
    out[pl.ds(0, left.shape[0])] = jnp.dot(
        left[...], factor[...], preferred_element_type=jnp.float32
    )


def mask_kernel(where, pattern, ranges, keep, give):
    block_row = pl.ds(lax.div(where[1] * NZ + where[2], BLK // 32), 1)
    count = M // BLK
    spread = (
        lax.broadcasted_iota(jnp.int32, (count, M), 0)
        == lax.div(lax.broadcasted_iota(jnp.int32, (count, M), 1), BLK)
    ).astype(jnp.bfloat16)
    for b, (out, at) in enumerate(((keep, 0), (give, 0), (keep, 1), (give, 1))):
        present = pattern[b, block_row, :].astype(jnp.float32).astype(jnp.bfloat16)
        mask = jnp.dot(present, spread, preferred_element_type=jnp.float32)
        out[at] = ranges[b] * mask


VMEM = pl.BlockSpec(memory_space=pltpu.VMEM)
SMEM = pl.BlockSpec(memory_space=pltpu.SMEM)


def masked(where, pattern, ranges):
    return pl.pallas_call(
        mask_kernel,
        out_shape=[jax.ShapeDtypeStruct((2, 32, M), jnp.float32)] * 2,
        in_specs=[SMEM, VMEM, VMEM],
        out_specs=[VMEM, VMEM],
        compiler_params=pltpu.CompilerParams(vmem_limit_bytes=8 << 20),
        name="masked",
    )(where, pattern, ranges)


def chain_kernel(where, keep, other, *refs):
    parts, (out, first, second, left, prod, sums) = refs[:PARTS], refs[PARTS:]
    order(where, parts, first, second)

    @pl.when(where[0] == 1)
    def _():
        half = jnp.bfloat16
        down, up = keep[1].astype(jnp.float32), other[0].astype(jnp.float32)
        left[pl.ds(0, 32)] = down.astype(half)
        left[pl.ds(32, 32)] = up.astype(half)
        wide_dot(left, second, prod)
        reach = prod[pl.ds(0, 32)]
        left[pl.ds(0, 32)] = reach.astype(half)
        sums[pl.ds(0, 32)] = reach
        sums[pl.ds(32, 32)] = up
        sums[pl.ds(64, 32)] = down
        sums[pl.ds(96, 32)] = jnp.zeros((32, M), jnp.float32)

        @pl.loop(0, 4)
        def _(n):
            wide_dot(left, first, prod)
            sums[pl.ds(64, 64)] += prod[...]
            left[...] = prod[...].astype(half)
            wide_dot(left, second, prod)
            sums[pl.ds(0, 32)] += prod[pl.ds(0, 32)]

            @pl.when(n < 3)
            def _():
                sums[pl.ds(32, 32)] += prod[pl.ds(32, 32)]

            left[...] = prod[...].astype(half)

        out[...] = sums[...].astype(half)


def chain(where, keep, other, parts):
    return pl.pallas_call(
        chain_kernel,
        out_shape=[
            jax.ShapeDtypeStruct((128, M), jnp.bfloat16),
            jax.ShapeDtypeStruct((M, M), jnp.bfloat16),
            jax.ShapeDtypeStruct((M, M), jnp.bfloat16),
        ],
        in_specs=[SMEM] + [VMEM] * (2 + PARTS),
        out_specs=[VMEM] * 3,
        scratch_shapes=[
            pltpu.VMEM((64, M), jnp.bfloat16),
            pltpu.VMEM((64, M), jnp.float32),
            pltpu.VMEM((128, M), jnp.float32),
        ],
        compiler_params=pltpu.CompilerParams(vmem_limit_bytes=20 << 20),
        name="chain",
    )(where, keep, other, *parts)


def finish_kernel(last, where, lefts, keep, other, first, second, *refs):
    outs, prod = refs[:-1], refs[-1]

    @pl.when(where[0] == 0)
    def _():
        wide_dot(lefts.at[pl.ds(0, 64)], first, prod.at[0])
        wide_dot(lefts.at[pl.ds(64, 64)], second, prod.at[1])
        top = keep[0].astype(jnp.float32) + prod[1, pl.ds(32, 32)]
        up = prod[0, pl.ds(32, 32)]
        down = prod[1, pl.ds(0, 32)]
        bottom = other[1].astype(jnp.float32) + prod[0, pl.ds(0, 32)]
        if last:
            for at, block in enumerate((top, up, down, bottom)):
                outs[0][at] = block
            return
        mine, mine_half, rest_half = outs
        for odd, pair, rest in ((0, (top, down), (up, bottom)), (1, (up, bottom), (top, down))):

            @pl.when(where[3] == odd)
            def _(pair=pair, rest=rest):
                for at in range(2):
                    mine[at] = pair[at]
                    mine_half[at] = pair[at].astype(jnp.bfloat16)
                    rest_half[at] = rest[at].astype(jnp.bfloat16)


def finish(last, where, lefts, keep, other, first, second):
    pair = (2, 32, M)
    if last:
        shapes = [jax.ShapeDtypeStruct((4, 32, M), jnp.float32)]
    else:
        shapes = [
            jax.ShapeDtypeStruct(pair, kind) for kind in (jnp.float32, jnp.bfloat16, jnp.bfloat16)
        ]
    return pl.pallas_call(
        functools.partial(finish_kernel, last),
        out_shape=shapes,
        in_specs=[SMEM] + [VMEM] * 5,
        out_specs=[VMEM] * len(shapes),
        scratch_shapes=[pltpu.VMEM((2, 64, M), jnp.float32)],
        compiler_params=pltpu.CompilerParams(vmem_limit_bytes=16 << 20),
        name="finish",
    )(where, lefts, keep, other, first, second)


def star(last, where, keep, other):
    block = jnp.where(
        where[0] == 1,
        jnp.concatenate([keep[0], other[1]]),
        jnp.concatenate([other[0], keep[1]]),
    ).astype(jnp.bfloat16)
    parts_a, parts_b = gather(block)
    sums, first, second = chain(where, keep, other, parts_a + parts_b)
    lefts = send(sums, lambda x, c, y, z: (x, 0, y, z) if c == 1 else None)
    return finish(last, where, lefts, keep, other, first, second)


def body(ranges, pattern):
    slab = lax.axis_index("slab")
    panel = lax.axis_index("panel")
    core, odd = slab % NC, (slab // NC) % 2
    where = jnp.stack([core, panel // NZ, panel % NZ, odd]).astype(jnp.int32)

    keep, give = masked(where, pattern[0], ranges[0])
    other = send(give, lambda x, c, y, z: (x, 1 - c, y, z))
    mine, mine_half, rest_half = star(False, where, keep, other)

    near = send(rest_half, lambda x, c, y, z: (x, 1, y, z) if c == 0 else None)
    far = send(
        jnp.where(core == 0, mine_half, near), lambda x, c, y, z: (x ^ 1, c, y, z)
    ).astype(jnp.float32)
    local = jnp.where(core == 0, mine, near.astype(jnp.float32))
    swap = (odd == 1) == (core == 0)
    keep, other = jnp.where(swap, far, local), jnp.where(swap, local, far)
    (joint,) = star(True, where, keep, other)
    shared = send(joint, lambda x, c, y, z: (x, 1, y, z) if c == 0 else None)
    return jnp.where(core == 1, shared, joint)[None]


def solution(mesh):
    return jax.shard_map(
        body,
        mesh=mesh,
        in_specs=(P("slab", None, "panel", None), P("slab", None, None, None)),
        out_specs=P("slab", None, "panel", None),
        check_vma=False,
    )
```
